32 devices in a mesh: pipe: 4 (over y, x), dp: 8 (over z, core).
Axes of the slice: x: 2, y: 2, z: 4, core: 2. Of those that a mesh axis runs over, the one named last changes fastest.
Arguments:
- source: bfloat16 [16, 1024, 512], P('dp', 'pipe'), may hold values from -6 to 6
- target: bfloat16 [16, 1024, 512], P('dp', 'pipe'), may hold values from -6 to 6
- source_length: int32 [16], P('dp'), may hold values from 128 to 1024, as said below
- target_length: int32 [16], P('dp'), may hold values from 128 to 1024, as said below
- memory_cotangent: bfloat16 [16, 1024, 512], P('dp', 'pipe'), may hold values from -6 to 6
- output_cotangent: bfloat16 [16, 1024, 512], P('dp', 'pipe'), may hold values from -6 to 6
- source_query: bfloat16 [512, 512], replicated, may hold values from -0.25 to 0.25
- source_keyvalue: bfloat16 [512, 1024], replicated, may hold values from -0.25 to 0.25
- source_output: bfloat16 [512, 512], replicated, may hold values from -3 to 3
- source_gain: float32 [512], replicated, may hold values from 0.25 to 1.75
- source_offset: float32 [512], replicated, may hold values from -3 to 3
- source_expand: bfloat16 [512, 2048], replicated, may hold values from -0.25 to 0.25
- source_bias: float32 [2048], replicated, may hold values from -3 to 3
- source_contract: bfloat16 [2048, 512], replicated, may hold values from -0.125 to 0.125
- source_shift: float32 [512], replicated, may hold values from -3 to 3
- source_scale: float32 [512], replicated, may hold values from 0.25 to 1.75
- source_center: float32 [512], replicated, may hold values from -3 to 3
- target_query: bfloat16 [512, 512], replicated, may hold values from -0.25 to 0.25
- target_keyvalue: bfloat16 [512, 1024], replicated, may hold values from -0.25 to 0.25
- target_output: bfloat16 [512, 512], replicated, may hold values from -3 to 3
- target_gain: float32 [512], replicated, may hold values from 0.25 to 1.75
- target_offset: float32 [512], replicated, may hold values from -3 to 3
- cross_query: bfloat16 [512, 512], replicated, may hold values from -0.25 to 0.25
- cross_keyvalue: bfloat16 [512, 1024], replicated, may hold values from -0.25 to 0.25
- cross_output: bfloat16 [512, 512], replicated, may hold values from -3 to 3
- cross_gain: float32 [512], replicated, may hold values from 0.25 to 1.75
- cross_offset: float32 [512], replicated, may hold values from -3 to 3
- target_expand: bfloat16 [512, 2048], replicated, may hold values from -0.25 to 0.25
- target_bias: float32 [2048], replicated, may hold values from -3 to 3
- target_contract: bfloat16 [2048, 512], replicated, may hold values from -0.125 to 0.125
- target_shift: float32 [512], replicated, may hold values from -3 to 3
- target_scale: float32 [512], replicated, may hold values from 0.25 to 1.75
- target_center: float32 [512], replicated, may hold values from -3 to 3
Outputs:
- encoder_output: bfloat16 [16, 1024, 512], P('dp', 'pipe')
- decoder_output: bfloat16 [16, 1024, 512], P('dp', 'pipe')
- source_gradient: float32 [16, 1024, 512], P('dp', 'pipe')
- target_gradient: float32 [16, 1024, 512], P('dp', 'pipe')
- source_query_gradient: float32 [512, 512], P('dp')
- source_keyvalue_gradient: float32 [512, 1024], P('dp')
- source_output_gradient: float32 [512, 512], P('dp')
- source_gain_gradient: float32 [512], P('dp')
- source_offset_gradient: float32 [512], P('dp')
- source_expand_gradient: float32 [512, 2048], P('dp')
- source_bias_gradient: float32 [2048], P('dp')
- source_contract_gradient: float32 [2048, 512], P('dp')
- source_shift_gradient: float32 [512], P('dp')
- source_scale_gradient: float32 [512], P('dp')
- source_center_gradient: float32 [512], P('dp')
- target_query_gradient: float32 [512, 512], P('dp')
- target_keyvalue_gradient: float32 [512, 1024], P('dp')
- target_output_gradient: float32 [512, 512], P('dp')
- target_gain_gradient: float32 [512], P('dp')
- target_offset_gradient: float32 [512], P('dp')
- cross_query_gradient: float32 [512, 512], P('dp')
- cross_keyvalue_gradient: float32 [512, 1024], P('dp')
- cross_output_gradient: float32 [512, 512], P('dp')
- cross_gain_gradient: float32 [512], P('dp')
- cross_offset_gradient: float32 [512], P('dp')
- target_expand_gradient: float32 [512, 2048], P('dp')
- target_bias_gradient: float32 [2048], P('dp')
- target_contract_gradient: float32 [2048, 512], P('dp')
- target_shift_gradient: float32 [512], P('dp')
- target_scale_gradient: float32 [512], P('dp')
- target_center_gradient: float32 [512], P('dp')
The draws below stay inside these ranges and needn't reach their ends.
Inputs may be any that keep to these rules, and one draw needn't show every extreme that they name: `source_length`: the number of real tokens of each source sequence; some sequence has all 1024. `target_length`: the number of real tokens of each target sequence; some sequence has all 1024.
All inputs are finite; a program needn't handle non-finite values.
Results may differ from the reference program's by a relative error of at most 0.024.
Values may be sent and summed in bfloat16 or wider, within the bound.
No kernel may reach another device: no remote copies, remote signals or barrier semaphores. Data moves between devices by JAX's collectives and lax.ppermute only.
A program may use at most 320 MiB of HBM per device.

```python
import jax
import jax.numpy as jnp
from jax import lax

D = 512
HEADS = 8
HEAD_DIM = 64
FF = 2048
SEQ_LEN = 1024
SEQS = 16


def lengths_from(key):
    first_key, second_key = jax.random.split(key)
    counts = jax.random.randint(first_key, (SEQS,), max(SEQ_LEN // 8, 1), SEQ_LEN + 1)
    longest = jax.random.randint(second_key, (), 0, SEQS)
    return counts.at[longest].set(SEQ_LEN).astype(jnp.int32)


def draw_source_length(key, part):
    key = jax.random.fold_in(key, 11)
    return lengths_from(key)


def draw_target_length(key, part):
    key = jax.random.fold_in(key, 12)
    return lengths_from(key)


def block_scale(own_key, shape, pieces, low, top_value):
    factor_of = 1.0
    for axis_at, blocks in pieces:
        heights = jax.random.uniform(jax.random.fold_in(jax.random.fold_in(own_key, 6), axis_at), (blocks,), jnp.float32, low / len(pieces), top_value / len(pieces))
        factor_of = factor_of * jnp.repeat(jnp.exp(heights), shape[axis_at] // blocks).reshape((-1,) + (1,) * (len(shape) - 1 - axis_at))
    return factor_of


def normal_values(key, extent, width, reach, cuts=(), held_as=jnp.bfloat16):
    loudness = block_scale(key, extent, cuts, -0.22, 0.18) if cuts else 1.0
    values = jax.random.normal(key, extent, jnp.float32) * width * loudness
    return jnp.minimum(jnp.maximum(values, -reach), reach).astype(held_as)


def setup_inputs(seed: int = 0) -> dict:
    streams_of = jax.random.split(jax.random.key(seed), 34)
    return {
        "source": normal_values(streams_of[0], (SEQS, SEQ_LEN, D), 1.0, 6.0, ((0, 8), (1, 4))),
        "target": normal_values(streams_of[1], (SEQS, SEQ_LEN, D), 1.0, 6.0, ((0, 8), (1, 4))),
        "source_length": draw_source_length(jax.random.fold_in(streams_of[33], 71), 0),
        "target_length": draw_target_length(jax.random.fold_in(streams_of[33], 71), 0),
        "memory_cotangent": normal_values(streams_of[4], (SEQS, SEQ_LEN, D), 1.0, 6.0, ((0, 8), (1, 4))),
        "output_cotangent": normal_values(streams_of[5], (SEQS, SEQ_LEN, D), 1.0, 6.0, ((0, 8), (1, 4))),
        "source_query": normal_values(streams_of[6], (D, D), D ** -0.5, 0.25),
        "source_keyvalue": normal_values(streams_of[7], (D, 2 * D), D ** -0.5, 0.25),
        "source_output": normal_values(streams_of[8], (D, D), (max(D // 128, 1)) ** -0.5, 3.0),
        "source_gain": jnp.clip(1.0 + 0.15 * jax.random.normal(streams_of[9], (D,), jnp.float32), 0.25, 1.75),
        "source_offset": normal_values(streams_of[10], (D,), 0.5, 3.0, (), jnp.float32),
        "source_expand": normal_values(streams_of[11], (D, FF), D ** -0.5, 0.25),
        "source_bias": normal_values(streams_of[12], (FF,), 0.5, 3.0, (), jnp.float32),
        "source_contract": normal_values(streams_of[13], (FF, D), FF ** -0.5, 0.125),
        "source_shift": normal_values(streams_of[14], (D,), 0.5, 3.0, (), jnp.float32),
        "source_scale": jnp.clip(1.0 + 0.15 * jax.random.normal(streams_of[15], (D,), jnp.float32), 0.25, 1.75),
        "source_center": normal_values(streams_of[16], (D,), 0.5, 3.0, (), jnp.float32),
        "target_query": normal_values(streams_of[17], (D, D), D ** -0.5, 0.25),
        "target_keyvalue": normal_values(streams_of[18], (D, 2 * D), D ** -0.5, 0.25),
        "target_output": normal_values(streams_of[19], (D, D), (max(D // 128, 1)) ** -0.5, 3.0),
        "target_gain": jnp.clip(1.0 + 0.15 * jax.random.normal(streams_of[20], (D,), jnp.float32), 0.25, 1.75),
        "target_offset": normal_values(streams_of[21], (D,), 0.5, 3.0, (), jnp.float32),
        "cross_query": normal_values(streams_of[22], (D, D), D ** -0.5, 0.25),
        "cross_keyvalue": normal_values(streams_of[23], (D, 2 * D), D ** -0.5, 0.25),
        "cross_output": normal_values(streams_of[24], (D, D), (max(D // 128, 1)) ** -0.5, 3.0),
        "cross_gain": jnp.clip(1.0 + 0.15 * jax.random.normal(streams_of[25], (D,), jnp.float32), 0.25, 1.75),
        "cross_offset": normal_values(streams_of[26], (D,), 0.5, 3.0, (), jnp.float32),
        "target_expand": normal_values(streams_of[27], (D, FF), D ** -0.5, 0.25),
        "target_bias": normal_values(streams_of[28], (FF,), 0.5, 3.0, (), jnp.float32),
        "target_contract": normal_values(streams_of[29], (FF, D), FF ** -0.5, 0.125),
        "target_shift": normal_values(streams_of[30], (D,), 0.5, 3.0, (), jnp.float32),
        "target_scale": jnp.clip(1.0 + 0.15 * jax.random.normal(streams_of[31], (D,), jnp.float32), 0.25, 1.75),
        "target_center": normal_values(streams_of[32], (D,), 0.5, 3.0, (), jnp.float32),
    }


@jax.custom_vjp
def low(v):
    return lax.optimization_barrier(v.astype(jnp.bfloat16)).astype(jnp.float32)

@jax.custom_vjp
def low_back(v):
    return v

def low_keep(v):
    return (low(v), None)

def low_pass(kept, grad):
    return (grad,)

def back_keep(v):
    return (v, None)

def back_low(kept, grad):
    return (low(grad),)
low.defvjp(low_keep, low_pass)
low_back.defvjp(back_keep, back_low)
HIGHEST = lax.Precision.HIGHEST

def rounded(value):
    return low(low_back(value))

def product(left, right):
    return jnp.dot(left, right, precision=HIGHEST)

def layer_norm(value, gain, offset):
    center = value - lax.optimization_barrier(jnp.mean(value, -1, keepdims=True))
    return center * lax.rsqrt(lax.optimization_barrier(jnp.mean(center * center, -1, keepdims=True)) + 1e-05) * gain + offset

def attention(query_rows, source_rows, key_count, causal, w_query, w_keyvalue, w_output):
    row_count, model_width = query_rows.shape
    queries = rounded(product(query_rows, w_query)).reshape(row_count, HEADS, HEAD_DIM)
    pairs = rounded(product(source_rows, w_keyvalue))
    keys = pairs[:, :model_width].reshape(-1, HEADS, HEAD_DIM)
    values = pairs[:, model_width:].reshape(-1, HEADS, HEAD_DIM)
    block = min(512, row_count)
    query_blocks = queries.reshape(row_count // block, block, HEADS, HEAD_DIM)
    starts = jnp.arange(row_count // block, dtype=jnp.int32) * block
    key_places = jnp.arange(keys.shape[0], dtype=jnp.int32)

    def one_block(inputs):
        query_block, start = inputs
        scores = low_back(jnp.einsum('qhd,khd->hqk', query_block, keys, precision=HIGHEST) * HEAD_DIM ** (-0.5))
        allowed = key_places[None, :] < key_count
        if causal:
            query_places = start + jnp.arange(block, dtype=jnp.int32)
            allowed = allowed & (key_places[None, :] <= query_places[:, None])
        probs = jax.nn.softmax(jnp.where(allowed[None], scores, -1000000000.0), axis=-1)
        return jnp.einsum('hqk,khd->qhd', low(probs), values, precision=HIGHEST)
    mixed = lax.map(jax.checkpoint(one_block), (query_blocks, starts))
    mixed = rounded(mixed.reshape(row_count, model_width))
    return low_back(product(mixed, w_output))

def feedforward(hidden, residual, w_expand, b_expand, w_contract, b_contract, gain, offset):
    before = low_back(product(hidden, w_expand) + b_expand)
    active = rounded(jax.nn.gelu(before, approximate=True))
    branch = low_back(product(active, w_contract) + b_contract)
    return layer_norm(hidden + branch + residual, gain, offset)

def layers_forward(source_rows, target_rows, source_count, target_count, weights):
    attended = attention(source_rows, source_rows, source_count, False, weights[0], weights[1], weights[2])
    hidden = rounded(layer_norm(source_rows + attended, weights[3], weights[4]))
    memory = low(feedforward(hidden, source_rows, weights[5], weights[6], weights[7], weights[8], weights[9], weights[10]))
    self_part = attention(target_rows, target_rows, target_count, True, weights[11], weights[12], weights[13])
    first = layer_norm(target_rows + self_part, weights[14], weights[15])
    cross_part = attention(low(first), low_back(memory), source_count, False, weights[16], weights[17], weights[18])
    second = rounded(layer_norm(first + cross_part, weights[19], weights[20]))
    output = low(feedforward(second, target_rows, weights[21], weights[22], weights[23], weights[24], weights[25], weights[26]))
    return (memory, output)

def reference(source, target, source_length, target_length, memory_cotangent, output_cotangent, source_query, source_keyvalue, source_output, source_gain, source_offset, source_expand, source_bias, source_contract, source_shift, source_scale, source_center, target_query, target_keyvalue, target_output, target_gain, target_offset, cross_query, cross_keyvalue, cross_output, cross_gain, cross_offset, target_expand, target_bias, target_contract, target_shift, target_scale, target_center):
    weights = tuple((weight.astype(jnp.float32) for weight in (source_query, source_keyvalue, source_output, source_gain, source_offset, source_expand, source_bias, source_contract, source_shift, source_scale, source_center, target_query, target_keyvalue, target_output, target_gain, target_offset, cross_query, cross_keyvalue, cross_output, cross_gain, cross_offset, target_expand, target_bias, target_contract, target_shift, target_scale, target_center)))

    def one_sequence(totals, inputs):
        source_rows, target_rows, source_count, target_count, memory_cot, output_cot = inputs

        def run(source_value, target_value, weight_values):
            return layers_forward(source_value, target_value, source_count, target_count, weight_values)
        results, pull = jax.vjp(run, source_rows.astype(jnp.float32), target_rows.astype(jnp.float32), weights)
        source_grad, target_grad, weight_grads = pull((memory_cot.astype(jnp.float32), output_cot.astype(jnp.float32)))
        totals = jax.tree.map(jnp.add, totals, weight_grads)
        return (totals, (results[0].astype(jnp.bfloat16), results[1].astype(jnp.bfloat16), source_grad, target_grad))
    zeros = jax.tree.map(jnp.zeros_like, weights)
    grads, stacked = lax.scan(one_sequence, zeros, (source, target, source_length, target_length, memory_cotangent, output_cotangent))
    return (stacked[0], stacked[1], stacked[2], stacked[3], grads[0], grads[1], grads[2], grads[3], grads[4], grads[5], grads[6], grads[7], grads[8], grads[9], grads[10], grads[11], grads[12], grads[13], grads[14], grads[15], grads[16], grads[17], grads[18], grads[19], grads[20], grads[21], grads[22], grads[23], grads[24], grads[25], grads[26])
```

```python
import functools

import jax
import jax.numpy as jnp
from jax import lax
from jax.experimental import pallas as pl
from jax.experimental.pallas import tpu as pltpu
from jax.sharding import PartitionSpec as P

HEAD_DIM = 64
PAIR = 2 * HEAD_DIM
LOG2E = 1.4426950408889634
LN2 = 0.6931471805599453
HIDDEN = -1e30
BF = jnp.bfloat16
F32 = jnp.float32
VMEM_BYTES = 56 * 2**20
SMALL_BYTES = 16 * 2**20


def product(left, right, sides):
    return lax.dot_general(left, right, (sides, ((), ())), preferred_element_type=F32)


def nn(left, right):
    return product(left, right, ((1,), (0,)))


def nt(left, right):
    return product(left, right, ((1,), (1,)))


def tn(left, right):
    return product(left, right, ((0,), (0,)))


def norm_forward(value):
    center = value - jnp.mean(value, -1, keepdims=True)
    inverse = lax.rsqrt(jnp.mean(center * center, -1, keepdims=True) + 1e-05)
    return center * inverse, inverse


def norm_backward(gradient, normed, inverse, gain):
    scaled = gradient * gain
    back = inverse * (
        scaled
        - jnp.mean(scaled, -1, keepdims=True)
        - normed * jnp.mean(scaled * normed, -1, keepdims=True)
    )
    return (
        back,
        jnp.sum(gradient * normed, 0, keepdims=True),
        jnp.sum(gradient, 0, keepdims=True),
    )


def fill_bias(place_ref, count, causal, bias_ref):
    keys, width = bias_ref.shape
    rows = keys // 4
    for block in range(4):
        first = block * rows if causal else place_ref[block]
        at = first + lax.broadcasted_iota(jnp.int32, (rows, width), 0)
        allowed = at < count
        if causal:
            lane = lax.broadcasted_iota(jnp.int32, (rows, width), 1)
            asked = jnp.where(lane < rows, place_ref[0] + lane, place_ref[1] + lane - rows)
            allowed = allowed & (at <= asked)
        bias_ref[block * rows : (block + 1) * rows, :] = jnp.where(allowed, 0.0, HIDDEN)


def by_core(place_ref, rows, keys, run):
    block = rows // 2
    for core in range(2):
        seen = (core + 1, keys // block - core)

        @pl.when(place_ref[6] == core)
        def _(seen=seen):
            run(tuple((at * block, (at + 1) * block, count * block) for at, count in enumerate(seen)))


def bias_of(bias_ref, first, last, keys):
    width = bias_ref.shape[1]
    if width > 128:
        return bias_ref[:keys, first:last]
    return jnp.concatenate([bias_ref[:keys, :]] * ((last - first) // width), 1)


def head_lanes(half):
    lane = lax.broadcasted_iota(jnp.int32, (1, PAIR), 1)
    return (lane >= HEAD_DIM * half) & (lane < HEAD_DIM * (half + 1))


def project(own, other_ref, wq, wkv, q_ref, k_ref, v_ref, own_keys=None, starts=None):
    rows, width = own.shape
    q_ref[...] = (nn(own, wq[...]) * (HEAD_DIM**-0.5 * LOG2E)).astype(BF)
    keys = own if own_keys is None else own_keys
    for at in (0, rows):
        for ref, part in ((k_ref, wkv[:, :width]), (v_ref, wkv[:, width:])):
            value = nn(keys, part).astype(BF)
            if starts is None:
                ref[at : at + rows, :] = value
                continue
            block = rows // 2
            for half in range(2):
                first = pl.multiple_of(starts[2 * at // rows + half], block)
                ref[pl.ds(first, block), :] = value[half * block : (half + 1) * block]
        keys = other_ref[...]


def attend(spans, step, q_ref, k_ref, v_ref, bias_ref, ot_ref, lse_ref):
    def one_head(index, half):
        cols = pl.ds(pl.multiple_of(index // 2 * PAIR, PAIR), PAIR)
        at = pl.multiple_of(index * HEAD_DIM, HEAD_DIM)
        values = v_ref[:, cols].T
        if isinstance(half, int):
            values = values[HEAD_DIM * half : HEAD_DIM * (half + 1)]
        else:
            values = jnp.where(half == 0, values[:HEAD_DIM], values[HEAD_DIM:])
        for first, last, seen in spans:
            queries, keys = q_ref[first:last, cols], k_ref[:seen, cols]
            masked = jnp.where(head_lanes(half), queries, jnp.zeros_like(queries))
            scores = nt(keys, masked) + bias_of(bias_ref, first, last, seen)
            top = jnp.max(scores, 0, keepdims=True)
            expon = jnp.exp2(scores - top)
            total = jnp.sum(expon, 0, keepdims=True)
            mixed = nn(values[:, :seen], expon.astype(BF))
            ot_ref[pl.ds(at, HEAD_DIM), first:last] = mixed / total
            lse_ref[pl.ds(index, 1), first:last] = top + jnp.log2(total)

    def heads(index, carry):
        for half in range(step):
            one_head(step * index + half, half if step == 2 else index % 2)
        return carry

    lax.fori_loop(0, q_ref.shape[1] // HEAD_DIM // step, heads, 0)


def attend_back(
    spans, q_ref, k_ref, v_ref, do_ref, bias_ref, lse_ref, delta_ref, dqt_ref, dk_ref, dv_ref
):
    def pair(index, carry):
        cols = pl.ds(pl.multiple_of(index * PAIR, PAIR), PAIR)
        turned = k_ref[:, cols].T
        done = 0
        for first, last, seen in spans:
            keys, values = k_ref[:seen, cols], v_ref[:seen, cols]
            queries, grads = q_ref[first:last, cols], do_ref[first:last, cols]
            dkeys = dvalues = None
            for half in range(2):
                mine = head_lanes(half)
                masked = jnp.where(mine, queries, jnp.zeros_like(queries))
                masked_grads = jnp.where(mine, grads, jnp.zeros_like(grads))
                head = pl.ds(2 * index + half, 1)
                scores = nt(keys, masked) + bias_of(bias_ref, first, last, seen)
                probs = jnp.exp2(scores - lse_ref[head, first:last])
                dprobs = nt(values, masked_grads)
                dscores = (probs * (dprobs - delta_ref[head, first:last])).astype(BF)
                part = nn(probs.astype(BF), masked_grads)
                dvalues = part if half == 0 else dvalues + part
                part = nn(dscores, masked)
                dkeys = part if half == 0 else dkeys + part
                dquery = nn(turned[HEAD_DIM * half : HEAD_DIM * (half + 1), :seen], dscores)
                at = pl.multiple_of(index * PAIR + HEAD_DIM * half, HEAD_DIM)
                dqt_ref[pl.ds(at, HEAD_DIM), first:last] = (dquery * HEAD_DIM**-0.5).astype(BF)
            dkeys = dkeys * LN2
            if done:
                dkeys = jnp.concatenate([dkeys[:done] + dk_ref[:done, cols].astype(F32), dkeys[done:]], 0)
                dvalues = jnp.concatenate([dvalues[:done] + dv_ref[:done, cols].astype(F32), dvalues[done:]], 0)
            dk_ref[:seen, cols] = dkeys.astype(BF)
            dv_ref[:seen, cols] = dvalues.astype(BF)
            done = seen
        if done < k_ref.shape[0]:
            rest = jnp.zeros((k_ref.shape[0] - done, PAIR), BF)
            dk_ref[done:, cols] = rest
            dv_ref[done:, cols] = rest
        return carry

    lax.fori_loop(0, q_ref.shape[1] // PAIR, pair, 0)


class Spread:
    def __init__(self, core, keep_ref, send_ref):
        self.first = core == 0
        self.keep_ref, self.send_ref = keep_ref, send_ref
        self.quarters, self.planes, self.rows = keep_ref.shape[:3]

    def put(self, quarter, plane, at, even, odd):
        even, odd = even.astype(BF), odd.astype(BF)
        rows = slice(at, at + even.shape[0])
        self.keep_ref[quarter, plane, rows, :] = jnp.where(self.first, even, odd)
        self.send_ref[quarter, plane, rows, :] = jnp.where(self.first, odd, even)

    def square(self, value, at):
        chunk = value.shape[0] // (2 * self.planes)
        piece = chunk // self.quarters
        for plane in range(self.planes):
            for quarter in range(self.quarters):
                even = 2 * plane * chunk + quarter * piece
                odd = even + chunk
                self.put(quarter, plane, at, value[even : even + piece], value[odd : odd + piece])

    def columns(self, value, quarter, at):
        chunk = value.shape[0] // (2 * self.planes)
        for plane in range(self.planes):
            even = 2 * plane * chunk
            odd = even + chunk
            self.put(quarter, plane, at, value[even : even + chunk], value[odd : odd + chunk])

    def two_chunks(self, value, plane, at):
        chunk = value.shape[0] // 2
        piece = chunk // self.quarters
        for quarter in range(self.quarters):
            even = quarter * piece
            odd = even + chunk
            self.put(quarter, plane, at, value[even : even + piece], value[odd : odd + piece])

    def same(self, quarter, at, value):
        for plane in range(self.planes):
            self.put(quarter, plane, at, value, value)


class Chunks(Spread):
    def __init__(self, ref):
        self.ref = ref
        self.quarters, self.planes, self.rows = ref.shape[1], ref.shape[0] // 2, ref.shape[2]

    def put(self, quarter, plane, at, even, odd):
        rows = slice(at, at + even.shape[0])
        self.ref[2 * plane, quarter, rows, :] = even.astype(BF)
        self.ref[2 * plane + 1, quarter, rows, :] = odd.astype(BF)


class Whole:
    def __init__(self, refs):
        self.refs = refs


def spread_of(io, refs):
    if isinstance(refs, list) and len(refs) == 2:
        return Spread(io.place[6], *refs)
    if isinstance(refs, list):
        return Whole(refs)
    return Chunks(refs)


def spread_attention(spread, own, keys_own, keys_other, dar, ot_ref, dqt_ref, dk, dv):
    rows, width = dar.shape
    dq = dqt_ref[...].T
    own_t = own[...].T
    keys_t = own_t if keys_own is own else keys_own[...].T
    other_t = keys_other[...].T
    dwo = nn(ot_ref[...].astype(BF), dar)
    dwq = nn(own_t, dq)
    dwk = nn(keys_t, dk[0]) + nn(other_t, dk[1])
    dwv = nn(keys_t, dv[0]) + nn(other_t, dv[1])
    if isinstance(spread, Whole):
        wq_ref, wkv_ref, wo_ref = spread.refs
        wq_ref[...] = dwq.astype(BF)
        wkv_ref[:, :width] = dwk.astype(BF)
        wkv_ref[:, width:] = dwv.astype(BF)
        wo_ref[...] = dwo.astype(BF)
        return
    piece = spread.rows // 4
    for place, value in enumerate((dwq, dwk, dwv, dwo)):
        spread.square(value, place * piece)


BLOCK = 512
TANH_SCALE = 0.7978845608028654
TANH_CUBE = 0.044715


def expand(hidden, w1, b1, active_ref, slope_ref):
    for at in range(0, w1.shape[1], BLOCK):
        cols = slice(at, at + BLOCK)
        before = nn(hidden, w1[:, cols]) + b1[:, cols]
        square = before * before
        inner = before * (TANH_SCALE + (TANH_SCALE * TANH_CUBE) * square)
        curve = jnp.tanh(inner)
        half = 0.5 * (1.0 + curve)
        active_ref[:, cols] = (before * half).astype(BF)
        steep = TANH_SCALE + (3 * TANH_SCALE * TANH_CUBE) * square
        slope_ref[:, cols] = (half + (0.5 * before) * (1.0 - curve * curve) * steep).astype(BF)


def contract(hidden, residual, active_ref, w2, b2):
    total = hidden.astype(F32) + nn(active_ref[...], w2[...]) + b2[...] + residual.astype(F32)
    return norm_forward(total)


def ffn_backward(io, spread, back, hidden, parts, bias_grad_ref):
    low = back.astype(BF)
    hidden_t = hidden.T
    dhidden = None
    for number in range(bias_grad_ref.shape[0]):
        w1, w2, active, slope = parts(number)
        dactive = nt(low, w2).astype(BF)
        dbefore = (dactive.astype(F32) * slope.astype(F32)).astype(BF)
        bias_grad_ref[number : number + 1, :] = jnp.sum(dbefore.astype(F32), 0, keepdims=True)
        dcontract = tn(active, low)
        dexpand = nn(hidden_t, dbefore)
        if isinstance(spread, Whole):
            block = slice(number * BLOCK, (number + 1) * BLOCK)
            spread.refs[0][:, block] = dexpand.astype(BF)
            spread.refs[1][block, :] = dcontract.astype(BF)
        else:
            chunk = dexpand.shape[0] // (2 * spread.planes)
            spread.columns(dexpand, number, 0)
            spread.two_chunks(dcontract, number, chunk)
            io.send_part(spread.ref, 2 * number, (slice(None), number, slice(0, chunk)))
            pair = slice(2 * number, 2 * number + 2)
            io.send_part(spread.ref, 2 * number + 1, (pair, slice(None), slice(chunk, 2 * chunk)))
        part = nt(dbefore, w1)
        dhidden = part if dhidden is None else dhidden + part
    return dhidden, jnp.sum(low.astype(F32), 0, keepdims=True)


PARTS = 12


class Buffers:
    def __init__(self, place, ins, outs, small):
        self.place, self.ins, self.outs, self.small = place, ins, outs, small
        self.waiting, self.going = {}, []
        self.queue, late = [], []
        for name, entry in ins.items():
            if entry is None:
                self.ahead()
                continue
            buffer, sources, sems = entry
            copies = [
                pltpu.make_async_copy(source, buffer.at[where], sems.at[number])
                for number, (source, where) in enumerate(sources)
            ]
            self.waiting[name] = copies
            if len(copies) > 2:
                late.append(copies)
            else:
                self.queue += copies
        for copies in zip(*late, strict=True):
            self.queue += copies
        if None not in ins.values():
            self.ahead()
        self.sent = set()

    def __getattr__(self, name):
        if name in self.small:
            return self.small[name]
        if name in self.outs:
            buffers = self.outs[name]
            return [buffer for buffer, _, _ in buffers] if isinstance(buffers, list) else buffers[0]
        for copy in self.waiting[name]:
            self.wait(copy)
        self.waiting[name] = []
        return self.ins[name][0]

    def block(self, name, number):
        self.wait(self.waiting[name][number])
        if number + 1 == len(self.waiting[name]):
            self.waiting[name] = []
        return self.ins[name][0]

    def ahead(self):
        for copy in self.queue:
            copy.start()
        self.queue = []

    def wait(self, copy):
        if any(copy is other for other in self.queue):
            self.ahead()
        copy.wait()

    def results(self):
        for entry in self.outs.values():
            yield from entry if isinstance(entry, list) else [entry]

    def start(self, copy):
        copy.start()
        self.going.append(copy)

    def send(self, *refs):
        for buffer, targets, sems in self.results():
            if any(buffer is ref for ref in refs):
                self.sent.add(id(buffer))
                for number, (target, where) in enumerate(targets):
                    self.start(pltpu.make_async_copy(buffer.at[where], target, sems.at[number]))

    def send_part(self, ref, number, where):
        for buffer, targets, sems in self.results():
            if buffer is ref:
                self.sent.add(id(buffer))
                self.start(
                    pltpu.make_async_copy(buffer.at[where], targets[0][0].at[where], sems.at[number])
                )

    def finish(self):
        self.send(*[entry[0] for entry in self.results() if id(entry[0]) not in self.sent])
        for copies in self.waiting.values():
            for copy in copies:
                self.wait(copy)
        for copy in self.going:
            copy.wait()


class Part:
    def __init__(self, io, prefix):
        self.io, self.prefix = io, prefix
        self.place, self.send, self.ahead = io.place, io.send, io.ahead

    def __getattr__(self, name):
        return getattr(self.io, self.prefix + name)


class Ends(list):
    pass


class Blocks:
    def __init__(self, array, axis):
        self.array, self.axis = array, axis


def run(kernel, name, flops, place, ins, small, outs, scratch=()):
    arrays, buffers, sem_counts, shapes = [], [], [], []
    in_plan, out_plan = {}, {}

    def buffer(dims, dtype, sems):
        buffers.append(pltpu.VMEM(tuple(dims), dtype))
        sem_counts.append(sems)
        return len(buffers) - 1

    for key, value in ins.items():
        if value is None:
            in_plan[key] = None
            continue
        plan = []
        if isinstance(value, Blocks):
            array, axis = value.array, value.axis
            for at in range(0, array.shape[axis], BLOCK):
                where = (slice(None),) * axis + (slice(at, at + BLOCK),)
                plan.append((len(arrays), where, where))
            arrays.append(array)
            dims, dtype = array.shape, array.dtype
        else:
            rows = 0
            for part in value if isinstance(value, Ends) else [value]:
                array, index = part if isinstance(part, tuple) else (part, None)
                dims = array.shape if index is None else array.shape[1:]
                where = len(plan) if isinstance(value, Ends) else ()
                plan.append((len(arrays), () if index is None else (index,), where))
                rows += dims[0]
                arrays.append(array)
            dims, dtype = (rows, *dims[1:]), array.dtype
        in_plan[key] = (buffer(dims, dtype, len(plan)), plan)

    def plan_out(value):
        if isinstance(value, Ends):
            plan = [(len(shapes) + number, number) for number in range(len(value))]
            shapes.extend(value)
            rows = sum(part.shape[0] for part in value)
            return buffer((rows, *value[0].shape[1:]), value[0].dtype, len(plan)), plan
        shapes.append(value)
        return buffer(value.shape, value.dtype, PARTS), [(len(shapes) - 1, ())]

    for key, value in outs.items():
        whole = isinstance(value, list) and not isinstance(value, Ends)
        out_plan[key] = [plan_out(part) for part in value] if whole else plan_out(value)

    def body(place_ref, *refs):
        cuts = (len(small), len(arrays), len(shapes), len(buffers), len(sem_counts))
        groups, at = [], 0
        for count in cuts:
            groups.append(refs[at : at + count])
            at += count
        small_refs, in_refs, out_refs, buffer_refs, sems = groups

        def part_of(ref, where):
            return ref.at[where] if where else ref

        def settled(where, rows):
            if not isinstance(where, int):
                return where
            return (pl.ds(pl.multiple_of((place_ref[9] ^ where) * rows, rows), rows),)

        def out_entry(plan):
            number, targets = plan
            return (
                buffer_refs[number],
                [(out_refs[which], settled(where, out_refs[which].shape[0])) for which, where in targets],
                sems[number],
            )

        def in_entry(number, plan):
            parts = []
            for which, where, to in plan:
                source = part_of(in_refs[which], where)
                parts.append((source, settled(to, source.shape[0])))
            return buffer_refs[number], parts, sems[number]

        in_map = {key: plan and in_entry(*plan) for key, plan in in_plan.items()}
        out_map = {
            key: [out_entry(part) for part in plan] if isinstance(plan, list) else out_entry(plan)
            for key, plan in out_plan.items()
        }
        io = Buffers(place_ref, in_map, out_map, dict(zip(small, small_refs, strict=True)))
        kernel(io, *refs[at:])
        io.finish()

    vmem, anywhere = pl.BlockSpec(memory_space=pltpu.VMEM), pl.BlockSpec(memory_space=pl.ANY)
    moved = sum(a.size * a.dtype.itemsize for a in (*arrays, *shapes))
    results = pl.pallas_call(
        body,
        out_shape=shapes,
        in_specs=[pl.BlockSpec(memory_space=pltpu.SMEM)] + [vmem] * len(small) + [anywhere] * len(arrays),
        out_specs=[anywhere] * len(shapes),
        scratch_shapes=[*buffers, *[pltpu.SemaphoreType.DMA((count,)) for count in sem_counts], *scratch],
        name=name,
        cost_estimate=pl.CostEstimate(flops=flops, bytes_accessed=moved, transcendentals=0),
        compiler_params=pltpu.CompilerParams(vmem_limit_bytes=VMEM_BYTES),
    )(place, *small.values(), *arrays)

    def named(plan):
        if isinstance(plan, list):
            return [named(part) for part in plan]
        got = [results[which] for which, _ in plan[1]]
        return got if len(got) > 1 else got[0]

    return Results({key: named(plan) for key, plan in out_plan.items()})


class Results(dict):
    def __getattr__(self, name):
        return self[name]


def put_norm(io, normed, inverse, normed_ref, inverse_ref):
    normed_ref[...] = normed
    inverse_ref[...] = jnp.broadcast_to(inverse, inverse_ref.shape)
    io.send(normed_ref, inverse_ref)


def self_attention(io, count_at, causal, bias_ref):
    fill_bias(io.place, io.place[count_at], causal, bias_ref)
    rows = io.own[...]
    starts = [io.place[block] for block in range(4)] if causal else None
    project(rows, io.other, io.wq, io.wkv, io.q, io.k, io.v, starts=starts)
    io.send(io.q, io.k, io.v)
    io.ahead()
    q, k, v, ot, lse = io.q, io.k, io.v, io.ot, io.lse
    run_spans(io, causal, lambda spans: attend(spans, 1 if causal else 2, q, k, v, bias_ref, ot, lse))
    io.send(ot, lse)
    return tn(ot[...].astype(BF), io.wo[...]), rows


def run_spans(io, causal, run):
    rows, keys = io.q.shape[0], io.k.shape[0]
    if causal:
        by_core(io.place, rows, keys, run)
    else:
        run(((0, rows, keys),))


def encoder_forward_kernel(io, bias_ref):
    attn, rows = self_attention(io, 4, False, bias_ref)
    normed, inverse = norm_forward(rows.astype(F32) + attn)
    put_norm(io, normed, inverse, io.n0, io.i0)
    hidden = (normed * io.gain[...] + io.offset[...]).astype(BF)
    io.hidden[...] = hidden
    io.send(io.hidden)
    expand(hidden, io.w1, io.b1, io.active, io.slope)
    io.send(io.active, io.slope)
    normed, inverse = contract(hidden, rows, io.active, io.w2, io.b2)
    io.memory[...] = (normed * io.scale[...] + io.center[...]).astype(BF)
    io.send(io.memory)
    put_norm(io, normed, inverse, io.n1, io.i1)


def decoder_forward_kernel(io, causal_ref, bias_ref, active_ref, slope_ref):
    attn, rows = self_attention(Part(io, "s"), 5, True, causal_ref)
    normed, inverse = norm_forward(rows.astype(F32) + attn)
    put_norm(io, normed, inverse, io.n, io.i)
    spread = spread_of(io, io.grads)
    fill_bias(io.place, io.place[4], False, bias_ref)
    first = io.n[...] * io.gain[...] + io.offset[...]
    first_low = first.astype(BF)
    io.first[...] = first_low
    io.send(io.first)
    memory = io.mem_own[...]
    project(first_low, io.mem_other, io.wq, io.wkv, io.q, io.k, io.v, memory)
    io.send(io.q, io.k, io.v)
    io.ahead()
    q, k, v, ot, lse = io.q, io.k, io.v, io.ot, io.lse
    run_spans(io, False, lambda spans: attend(spans, 1, q, k, v, bias_ref, ot, lse))
    io.send(io.ot, io.lse)
    n2, i2 = norm_forward(first + tn(io.ot[...].astype(BF), io.wo[...]))
    second = (n2 * io.cross_gain[...] + io.cross_offset[...]).astype(BF)
    expand(second, io.w1, io.b1, active_ref, slope_ref)
    n3, i3 = contract(second, io.sown[...], active_ref, io.w2, io.b2)
    output = (n3 * io.scale[...] + io.center[...]).astype(BF)
    block = output.shape[0] // 2
    for half in range(2):
        rows = slice(half * block, (half + 1) * block)
        io.result[2 * half] = memory[rows]
        io.result[2 * half + 1] = output[rows]
    io.send(io.result)
    back, dscale, dcenter = norm_backward(io.cotangent[...].astype(F32), n3, i3, io.scale[...])
    io.dr[...] = back
    io.send(io.dr)
    w1, w2 = io.w1, io.w2

    def parts(number):
        cut = slice(number * BLOCK, (number + 1) * BLOCK)
        return w1[:, cut], w2[cut, :], active_ref[:, cut], slope_ref[:, cut]

    vecs = io.vecs
    dhidden, dshift = ffn_backward(io, spread, back, second, parts, vecs.at[0:4])
    dsecond = (back + dhidden).astype(BF).astype(F32)
    dv2, dgain, doffset = norm_backward(dsecond, n2, i2, io.cross_gain[...])
    io.dv[...] = dv2
    io.send(io.dv)
    put_rows(vecs, 4, (dshift, dscale, dcenter, dgain, doffset))


def put_rows(ref, at, values):
    for row, value in enumerate(values):
        ref[at + row : at + row + 1, :] = value
    at += len(values)
    ref[at:, :] = jnp.zeros((ref.shape[0] - at, ref.shape[1]), F32)


def cross_backward_kernel(io, bias_ref, *scratch):
    fill_bias(io.place, io.place[4], False, bias_ref)
    dv2 = io.dv[...]
    du, dc_own, dc_other = attention_backward(
        io, False, bias_ref, scratch, dv2.astype(BF), "first", "mem_own", "mem_other"
    )
    io.dmem_other[...] = dc_other.astype(BF)
    io.dmem_own[...] = dc_own.astype(BF)
    io.send(io.dmem_other, io.dmem_own)
    dv1, dgain, doffset = norm_backward(dv2 + du, io.n[...], io.i[:, :1], io.gain[...])
    io.dv1[...] = dv1
    io.send(io.dv1)
    put_rows(io.vecs, 0, (dgain, doffset))


def self_backward(io, count_at, causal, bias_ref, scratch):
    fill_bias(io.place, io.place[count_at], causal, bias_ref)
    dv = io.dv[...]
    du, dc_own, dc_other = attention_backward(
        io, causal, bias_ref, scratch, dv.astype(BF), "own", "own", "other"
    )
    io.dc_other[...] = dc_other.astype(BF)
    io.send(io.dc_other)
    io.du[...] = (dv + io.extra[...] + du + dc_own).astype(BF)
    io.send(io.du)


def source_backward_kernel(io, bias_ref, *scratch):
    self_backward(io, 4, False, bias_ref, scratch)


def target_backward_kernel(io, bias_ref, *scratch):
    self_backward(io, 5, True, bias_ref, scratch)


def attention_backward(io, causal, bias_ref, scratch, dar, own, keys_own, keys_other):
    spread = spread_of(io, io.grads)
    do_ref, delta_ref, dqt_ref, dk_ref, dv_ref = scratch
    rows, width = dar.shape
    wo, ot = io.wo, io.ot
    do_ref[...] = nt(dar, wo[...]).astype(BF)
    turned = nt(wo[...], dar).astype(BF).astype(F32) * ot[...]
    delta_ref[...] = jnp.sum(turned.reshape(width // HEAD_DIM, HEAD_DIM, rows), 1)
    queries, keys, values, lse = io.q, io.k, io.v, io.lse
    io.ahead()
    run_spans(
        io,
        causal,
        lambda spans: attend_back(
            spans, queries, keys, values, do_ref, bias_ref, lse, delta_ref, dqt_ref, dk_ref, dv_ref
        ),
    )
    if causal:
        starts = [io.place[block] for block in range(4)]
        dk, dv = [
            [
                jnp.concatenate([ref[pl.ds(pl.multiple_of(first, rows // 2), rows // 2), :] for first in firsts], 0)
                for firsts in (starts[:2], starts[2:])
            ]
            for ref in (dk_ref, dv_ref)
        ]
    else:
        dk, dv = [[ref[:rows, :], ref[rows:, :]] for ref in (dk_ref, dv_ref)]
    own_ref = getattr(io, own)
    keys_ref = own_ref if keys_own == own else getattr(io, keys_own)
    spread_attention(spread, own_ref, keys_ref, getattr(io, keys_other), dar, ot, dqt_ref, dk, dv)
    io.send(*io.grads)
    dq = dqt_ref[...].T
    wkv = io.wkv
    dc = [
        nt(dk[at], wkv[:, :width]) + nt(dv[at], wkv[:, width:])
        for at in (1, 0)
    ]
    return nt(dq, io.wq[...]), dc[1], dc[0]


def encoder_ffn_backward(io):
    spread = spread_of(io, io.grads)
    dmemory = (io.dmem_own[...].astype(F32) + io.dmem_came[...].astype(F32)).astype(BF).astype(F32)
    total = io.cotangent[...].astype(F32) + dmemory
    back, dscale, dcenter = norm_backward(total, io.n1[...], io.i1[:, :1], io.scale[...])
    io.dr[...] = back
    io.send(io.dr)

    def parts(number):
        cut = slice(number * BLOCK, (number + 1) * BLOCK)
        return (
            io.block("w1", number)[:, cut],
            io.block("w2", number)[cut, :],
            io.block("active", number)[:, cut],
            io.block("slope", number)[:, cut],
        )

    vecs = io.vecs
    dhidden, dshift = ffn_backward(io, spread, back, io.hidden[...], parts, vecs.at[0:4])
    dlow = (back + dhidden).astype(BF).astype(F32)
    dv0, dgain, doffset = norm_backward(dlow, io.n0[...], io.i0[:, :1], io.gain[...])
    io.dv[...] = dv0
    io.send(io.dv)
    top, cross = io.top_vecs, io.cross_vecs
    rest = [top[row : row + 1, :] for row in range(9)] + [cross[row : row + 1, :] for row in range(2)]
    put_rows(vecs, 4, (dshift, dscale, dcenter, dgain, doffset, *rest))
    if not isinstance(spread, Whole):
        share = vecs.shape[0] // spread.quarters
        for quarter in range(spread.quarters):
            spread.same(quarter, spread.rows - share, vecs[quarter * share : (quarter + 1) * share, :])
        where = (slice(None), slice(None), slice(spread.rows - share, spread.rows))
        io.send_part(spread.ref, PARTS - 1, where)


def small_kernel(body, name, outs, place, *args):
    vmem = pl.BlockSpec(memory_space=pltpu.VMEM)
    moved = sum(a.size * a.dtype.itemsize for a in (*args, *outs))
    return pl.pallas_call(
        body,
        out_shape=outs,
        in_specs=[pl.BlockSpec(memory_space=pltpu.SMEM)] + [vmem] * len(args),
        out_specs=[vmem] * len(outs),
        name=name,
        cost_estimate=pl.CostEstimate(flops=0, bytes_accessed=moved, transcendentals=0),
        compiler_params=pltpu.CompilerParams(vmem_limit_bytes=SMALL_BYTES),
    )(place, *args)


def split_kernel(pairs, extra, place_ref, *refs):
    outs = refs[2 * pairs + extra :]
    for step, out_ref in enumerate(outs):
        quarter = place_ref[7] ^ step
        at = 0
        for plane in range(refs[0].shape[1]):
            for pair in range(pairs):
                keep_ref, came_ref = refs[2 * pair : 2 * pair + 2]
                rows = keep_ref.shape[2]
                total = keep_ref[quarter, plane].astype(F32) + came_ref[quarter, plane].astype(F32)
                out_ref[at : at + rows, :] = total.astype(BF)
                at += rows
        if extra:
            out_ref[at:, :] = refs[2 * pairs][quarter]


def split_pieces(place, pairs, extra=None):
    quarters, planes, _, width = pairs[0][0].shape
    rows = planes * sum(keep.shape[2] for keep, _ in pairs)
    args = [part for pair in pairs for part in pair]
    if extra is not None:
        rows += extra.shape[1]
        args.append(extra)
    body = functools.partial(split_kernel, len(pairs), int(extra is not None))
    outs = [jax.ShapeDtypeStruct((rows, width), BF)] * quarters
    return list(small_kernel(body, "split", outs, place, *args))


def join_kernel(place_ref, whole_ref, pieces_ref, *outs):
    rows = whole_ref.shape[0]
    for step, out_ref in enumerate(outs):
        out_ref[:rows, :] = whole_ref[...]
        out_ref[rows:, :] = pieces_ref[place_ref[7] ^ step]


def join_pieces(place, whole, pieces):
    outs = [jax.ShapeDtypeStruct((whole.shape[0] + pieces.shape[1], whole.shape[1]), BF)] * pieces.shape[0]
    return list(small_kernel(join_kernel, "join", outs, place, whole, pieces))


def home_kernel(place_ref, *refs):
    dus, came_refs, outs = (refs[:2], refs[2:4]), refs[4:6], refs[6:]
    rows = outs[0].shape[1]
    for which, out_ref in enumerate(outs):
        at = pl.multiple_of((place_ref[9] ^ which) * rows, rows)
        for number, (du, came_ref) in enumerate(zip(dus, came_refs, strict=True)):
            out_ref[number] = (du[which][...].astype(F32) + came_ref[pl.ds(at, rows), :].astype(F32)).astype(BF)


def home_blocks(place, source_du, source_came, target_du, target_came):
    outs = [jax.ShapeDtypeStruct((2, *source_du[0].shape), BF)] * 2
    return list(small_kernel(home_kernel, "home", outs, place, *source_du, *target_du, source_came, target_came))


def fold_kernel(sets, planes, place_ref, *refs):
    parts, outs = refs[:-planes], refs[-planes:]
    quarters, rows = len(parts) // sets, outs[0].shape[0] // sets
    for step, out_ref in enumerate(outs):
        plane = (place_ref[8] // 2) ^ step
        where = pl.ds(pl.multiple_of(plane * rows, rows), rows)
        for number in range(sets):
            of_set = parts[number * quarters : (number + 1) * quarters]
            total = sum(part[where, :].astype(F32) for part in of_set)
            out_ref[number * rows : (number + 1) * rows, :] = total.astype(BF)


def fold_pieces(place, sets, planes, height=None):
    total, width = sets[0][0].shape
    rows = len(sets) * (total if height is None else height) // planes
    outs = [jax.ShapeDtypeStruct((rows, width), BF)] * planes
    body = functools.partial(fold_kernel, len(sets), planes)
    return list(small_kernel(body, "fold", outs, place, *[part for parts in sets for part in parts]))


def unpack_kernel(plan, io):
    chip, group = io.place[7], io.place[8]
    pieces = [ref for key, ref in io.small.items()]
    if len(pieces) == 1:
        pieces = [(quarter, pieces[0].at[quarter]) for quarter in range(pieces[0].shape[0])]
    else:
        pieces = [(chip ^ step, ref) for step, ref in enumerate(pieces)]
    quarters = len(pieces)
    for quarter, piece_ref in pieces:
        width = piece_ref.shape[1]
        at = 0
        for kind, outs in plan:
            refs = getattr(io, outs)
            if kind == ATTENTION:
                size = refs[0].shape[0] // quarters
                rows = pl.ds(pl.multiple_of(quarter * size, size), size)
                values = [piece_ref[at + i * size : at + (i + 1) * size, :].astype(F32) for i in range(4)]
                refs[0][rows, :] = values[0]
                refs[1][rows, :width] = values[1]
                refs[1][rows, width:] = values[2]
                refs[2][rows, :] = values[3]
                at += 4 * size
            elif kind == FEEDFORWARD:
                size = refs[0].shape[0]
                cols = pl.ds(pl.multiple_of(quarter * width, width), width)
                refs[0][:, cols] = piece_ref[at : at + size, :].astype(F32)
                at += size
                size = refs[1].shape[0] // quarters
                rows = pl.ds(pl.multiple_of(quarter * size, size), size)
                refs[1][rows, :] = piece_ref[at : at + size, :].astype(F32)
                at += size
            else:
                size = piece_ref.shape[0] - at
                rows = pl.ds(pl.multiple_of(quarter * size, size), size)
                refs[0][rows, :] = piece_ref[at:, :].astype(F32)
    if kind == VECTORS:
        short = refs[1].shape[1]
        pair = refs[0][:, pl.ds(pl.multiple_of((group // 2) * 2 * short, 2 * short), 2 * short)]
        refs[1][...] = jnp.where(group % 2 == 0, pair[:, :short], pair[:, short:])


ATTENTION, FEEDFORWARD, VECTORS = range(3)


class Places:
    def __init__(self, quarters, groups):
        self.quarters, self.groups = quarters, groups
        self.sends = []
        for which in range(2):
            pairs = []
            for quarter in range(quarters):
                for group in range(groups):
                    plane, core = divmod(group, 2)
                    worker = self.chip_of(core, self.place_of(quarter) ^ which)
                    target = worker * groups + 2 * plane + self.group_of(quarter)
                    pairs.append((quarter * groups + group, target))
            self.sends.append(pairs)
        self.cores = [(group, group ^ 1) for group in range(groups)]

    def group_of(self, quarter):
        return (quarter ^ (quarter >> 1)) & 1

    def place_of(self, quarter):
        return quarter >> 1

    def chip_of(self, group, place):
        return 2 * place + (group ^ place)

    def order(self, rows, upper):
        return [jnp.where(upper, rows[1], rows[0]), jnp.where(upper, rows[0], rows[1])]

    def to_work(self, parts):
        return [
            lax.ppermute(part, ("pipe", "dp"), pairs)
            for part, pairs in zip(parts, self.sends, strict=True)
        ]

    def to_home(self, block_a, block_b):
        return [
            lax.ppermute(part, ("pipe", "dp"), pairs)
            for part, pairs in zip((block_a, block_b), self.sends, strict=True)
        ]

    def at_home(self, came, upper):
        first, second = came
        return jnp.stack([jnp.where(upper, second, first), jnp.where(upper, first, second)])

    def to_other_core(self, value):
        return lax.ppermute(value, "dp", self.cores)


def gate(*values):
    return list(lax.optimization_barrier(values))


def together(*values):
    return lax.optimization_barrier(values)


def after(results, *flying):
    kept, flying = lax.optimization_barrier((dict(results), flying))
    return Results(kept), *flying


def to_quarters(parts):
    quarters = len(parts)
    return [
        part if step == 0 else lax.ppermute(part, "pipe", [(i, i ^ step) for i in range(quarters)])
        for step, part in enumerate(parts)
    ]


def to_planes(parts):
    groups = 2 * len(parts)
    return [
        part if step == 0 else lax.ppermute(part, "dp", [(i, i ^ (2 * step)) for i in range(groups)])
        for step, part in enumerate(parts)
    ]


def total_of(parts):
    return sum(part.astype(F32) for part in parts).astype(BF)


def by_step(value, index):
    return [
        lax.dynamic_index_in_dim(value, index ^ step, 0, keepdims=False) for step in range(value.shape[0])
    ]


def shards(
    source, target, source_length, target_length, memory_cotangent, output_cotangent,
    source_query, source_keyvalue, source_output, source_gain, source_offset,
    source_expand, source_bias, source_contract, source_shift, source_scale, source_center,
    target_query, target_keyvalue, target_output, target_gain, target_offset,
    cross_query, cross_keyvalue, cross_output, cross_gain, cross_offset,
    target_expand, target_bias, target_contract, target_shift, target_scale, target_center,
):
    quarters, groups = lax.axis_size("pipe"), lax.axis_size("dp")
    chip, group = lax.axis_index("pipe"), lax.axis_index("dp")
    core, planes = group % 2, groups // 2
    micro, block, width = source.shape
    rows, keys = 2 * block, 4 * block
    heads = width // HEAD_DIM
    wide = source_expand.shape[1]
    spread = (width // groups) % (16 * quarters) == 0
    places = Places(quarters, groups)
    upper = chip >= quarters // 2
    swap = places.to_other_core

    lengths = jnp.stack([source_length, target_length])
    other_lengths = swap(lengths)
    own = places.to_work(places.order(source, upper))
    other = Ends(swap(part) for part in own)
    late = places.order(jnp.stack([target, output_cotangent, memory_cotangent], 1), upper)
    own, late = together(own, late)
    own = Ends(own)
    late = places.to_work(late)

    counts = jnp.where(core == places.group_of(chip), lengths, other_lengths)
    counts = lax.dynamic_index_in_dim(counts, places.place_of(chip), 1, keepdims=False)
    starts = [places.chip_of(which, at) * block for which in (core, 1 - core) for at in range(2)]
    slots = [*starts, counts[0], counts[1], core, chip, group, places.place_of(chip)]
    place = jnp.stack([jnp.asarray(slot, jnp.int32) for slot in slots])

    def row(vector):
        return vector.reshape(1, -1)

    def shape(*dims, dtype=BF):
        return jax.ShapeDtypeStruct(dims, dtype)

    half = shape(block, width)
    sheet = shape(rows, width, dtype=F32)
    lanes = shape(rows, 128, dtype=F32)
    saved = Results(
        q=shape(rows, width), k=shape(keys, width), v=shape(keys, width),
        ot=shape(width, rows, dtype=F32), lse=shape(heads, rows, dtype=F32),
    )
    flat_bias = pltpu.VMEM((keys, 128), F32)
    causal_bias = pltpu.VMEM((keys, rows), F32)
    back_scratch = [
        pltpu.VMEM((rows, width), BF), pltpu.VMEM((heads, rows), F32), pltpu.VMEM((width, rows), BF),
        pltpu.VMEM((keys, width), BF), pltpu.VMEM((keys, width), BF),
    ]
    vec_rows = 16 * quarters
    if spread:
        attn_rows = 4 * width // (groups * quarters)
        ffn_rows = 2 * wide // (groups * quarters)
        attention_grads = [shape(quarters, planes, attn_rows, width)] * 2
        top_grads = shape(groups, quarters, ffn_rows, width)
        source_ffn_grads = shape(groups, quarters, ffn_rows + vec_rows // quarters, width)
    else:
        attention_grads = [shape(width, cols) for cols in (width, 2 * width, width)]
        top_grads = [shape(width, wide), shape(wide, width), shape(16, 128)]
        source_ffn_grads = top_grads
    core_flops = 2 * 4 * rows * keys * width
    linear_flops = 2 * rows * width * width
    ffn_flops = 4 * rows * width * wide
    attn_flops = 2 * core_flops + 8 * linear_flops
    attn_back_flops = 5 * core_flops + 16 * linear_flops

    encoder = run(
        encoder_forward_kernel, "encoder", attn_flops + ffn_flops, place,
        dict(own=own, wq=source_query, other=other, wkv=source_keyvalue, rest=None, wo=source_output, w1=source_expand,
             w2=source_contract),
        dict(gain=row(source_gain), offset=row(source_offset), b1=row(source_bias), b2=row(source_shift),
             scale=row(source_scale), center=row(source_center)),
        dict(**saved, n0=sheet, i0=lanes, hidden=shape(rows, width), active=shape(rows, wide),
             slope=shape(rows, wide), n1=sheet, i1=lanes, memory=shape(rows, width)),
        [flat_bias],
    )
    *late, memory = gate(*late, encoder.memory)
    target_own = Ends((part, 0) for part in late)
    target_other = Ends(swap(part[0]) for part in late)
    memory_other = swap(memory)
    top = run(
        decoder_forward_kernel, "decoder", 2 * attn_flops + 3 * ffn_flops, place,
        dict(sown=target_own, swq=target_query, sother=target_other, swkv=target_keyvalue, rest=None, swo=target_output,
             wq=cross_query, mem_own=memory, mem_other=memory_other, wkv=cross_keyvalue, wo=cross_output,
             w1=target_expand, w2=target_contract, cotangent=Ends((part, 1) for part in late)),
        dict(gain=row(target_gain), offset=row(target_offset), cross_gain=row(cross_gain),
             cross_offset=row(cross_offset), b1=row(target_bias), b2=row(target_shift), scale=row(target_scale),
             center=row(target_center)),
        dict(sq=saved.q, sk=saved.k, sv=saved.v, sot=saved.ot, slse=saved.lse, n=sheet, i=lanes, **saved,
             first=shape(rows, width), result=Ends([shape(2, block, width)] * 2), dr=sheet, dv=sheet,
             vecs=shape(16, width, dtype=F32), grads=top_grads),
        [causal_bias, flat_bias, pltpu.VMEM((rows, wide), BF), pltpu.VMEM((rows, wide), BF)],
    )
    results = places.to_home(*top.result)
    if spread:
        top_total = lax.psum_scatter(top.grads, "dp", scatter_dimension=0, tiled=True)[0]

    def kept(results):
        return dict(ot=results.ot, k=results.k, q=results.q, v=results.v, lse=results.lse, rest=None)

    decoder = Results(ot=top.sot, k=top.sk, q=top.sq, v=top.sv, lse=top.slse)

    cross = run(
        cross_backward_kernel, "cross_back", attn_back_flops, place,
        dict(dv=top.dv, wo=cross_output, **kept(top), first=top.first, mem_own=memory, mem_other=memory_other,
             wkv=cross_keyvalue, wq=cross_query, n=top.n, i=top.i),
        dict(gain=row(target_gain)),
        dict(dmem_own=shape(rows, width), dmem_other=shape(rows, width), dv1=sheet, vecs=shape(8, width, dtype=F32),
             grads=attention_grads),
        [flat_bias, *back_scratch],
    )
    cross, results = after(cross, results)
    results = places.at_home(results, upper)
    dmem_came = swap(cross.dmem_other)
    cross_came = swap(cross.grads[1]) if spread else ()
    target_back = run(
        target_backward_kernel, "target_back", attn_back_flops, place,
        dict(dv=cross.dv1, wo=target_output, **kept(decoder), own=target_own, other=target_other,
             wkv=target_keyvalue, wq=target_query, extra=top.dr),
        {}, dict(dc_other=shape(rows, width), du=Ends([half, half]), grads=attention_grads),
        [causal_bias, *back_scratch],
    )
    target_back, dmem_came, cross_came = after(target_back, dmem_came, cross_came)
    dtarget_came = swap(target_back.dc_other)
    target_came, early = (), ()
    if spread:
        target_came = swap(target_back.grads[1])
        early = split_pieces(place, [(cross.grads[0], cross_came)])
        early, dmem_came = together(early, dmem_came)
        early = to_quarters(early)
    source_ffn = run(
        encoder_ffn_backward, "source_ffn", 2 * ffn_flops, place,
        dict(cotangent=Ends((part, 2) for part in late), dmem_own=cross.dmem_own, dmem_came=dmem_came,
             n1=encoder.n1, i1=encoder.i1, w2=Blocks(source_contract, 0), slope=Blocks(encoder.slope, 1),
             w1=Blocks(source_expand, 1), active=Blocks(encoder.active, 1), hidden=encoder.hidden, n0=encoder.n0,
             i0=encoder.i0),
        dict(scale=row(source_scale), gain=row(source_gain), top_vecs=top.vecs, cross_vecs=cross.vecs),
        dict(dr=sheet, dv=sheet, vecs=shape(vec_rows, width, dtype=F32), grads=source_ffn_grads),
    )
    source_ffn, dtarget_came, target_came, early = after(source_ffn, dtarget_came, target_came, early)
    dv0, middle = source_ffn.dv, ()
    if spread:
        source_total = lax.psum_scatter(source_ffn.grads, "dp", scatter_dimension=0, tiled=True)[0]
        middle = split_pieces(place, [(target_back.grads[0], target_came)], top_total)
        dv0, middle = together(dv0, middle)
        middle = to_quarters(middle)
    source_back = run(
        source_backward_kernel, "source_back", attn_back_flops, place,
        dict(dv=dv0, wo=source_output, **kept(encoder), own=own, other=other, wkv=source_keyvalue,
             wq=source_query, extra=source_ffn.dr),
        {}, dict(dc_other=shape(rows, width), du=Ends([half, half]), grads=attention_grads),
        [flat_bias, *back_scratch],
    )
    source_back, middle = after(source_back, middle)

    def attention_outs():
        chunk = width // groups
        return [shape(chunk, width, dtype=F32), shape(chunk, 2 * width, dtype=F32), shape(chunk, width, dtype=F32)]

    def ffn_outs():
        return [shape(width // groups, wide, dtype=F32), shape(wide // groups, width, dtype=F32)]

    def unpack(name, plan, parts, outs):
        return run(
            functools.partial(unpack_kernel, plan), name, 0, place, {}, dict(enumerate(parts)), outs
        )

    dsource_came = swap(source_back.dc_other)
    blocks = (source_back.du, dsource_came, target_back.du, dtarget_came)
    if spread:
        last_came = swap(source_back.grads[1])
        last = split_pieces(place, [(source_back.grads[0], last_came)])
        height = planes * attn_rows
        last, home = together(last, home_blocks(place, *blocks))
        last, home = to_quarters(last), places.to_home(*home)
        first = total_of([part[height:] for part in middle])
        both = to_planes(fold_pieces(place, [early, middle, last], planes, height))
        pieces = to_quarters(join_pieces(place, first, source_total))
        both, pieces, home = together(both, pieces, home)
        first = pieces
        pieces = [part[ffn_rows:] for part in pieces]
        last = [jnp.concatenate([total_of(both), total_of(pieces)], 0)] * quarters
        last = to_quarters(last)
    else:
        home = places.to_home(*home_blocks(place, *blocks))
    gradients = places.at_home(home, upper).astype(F32)
    if spread:
        first_grads = unpack(
            "unpack_first", ((FEEDFORWARD, "top"),), first, dict(top=ffn_outs()),
        )
        last_grads = unpack(
            "unpack_last",
            (
                (ATTENTION, "cross"), (ATTENTION, "target"), (ATTENTION, "source"), (FEEDFORWARD, "low"),
                (VECTORS, "vectors"),
            ),
            last,
            dict(cross=attention_outs(), target=attention_outs(), source=attention_outs(), low=ffn_outs(),
                 vectors=[shape(vec_rows, width, dtype=F32), shape(vec_rows, width // groups, dtype=F32)]),
        )
        vectors, thin = last_grads.vectors
        source_attn, target_attn, cross_attn = last_grads.source, last_grads.target, last_grads.cross
        source_wide, target_wide = last_grads.low, first_grads.top
    else:
        vectors = lax.psum(source_ffn.vecs, ("pipe", "dp"))
        thin = lax.dynamic_slice_in_dim(vectors, group * (width // groups), width // groups, 1)

        def reduced(parts):
            flat = jnp.concatenate([part.reshape(groups, -1) for part in parts], 1)
            total = lax.psum(lax.psum_scatter(flat, "dp", scatter_dimension=0, tiled=True)[0], "pipe")
            outs, at = [], 0
            for part in parts:
                size = part.size // groups
                outs.append(total[at : at + size].reshape(-1, part.shape[1]).astype(F32))
                at += size
            return outs

        source_attn, target_attn, cross_attn = [
            reduced(results.grads) for results in (source_back, target_back, cross)
        ]
        source_wide, target_wide = [reduced(results.grads[:2]) for results in (source_ffn, top)]

    def bias(first_row):
        whole = vectors[first_row : first_row + wide // width].reshape(groups, -1)
        return lax.dynamic_index_in_dim(whole, group, 0, keepdims=False)

    return (
        results[:, 0], results[:, 1], gradients[:, 0], gradients[:, 1],
        *source_attn, thin[7], thin[8],
        source_wide[0], bias(0), source_wide[1], thin[4], thin[5], thin[6],
        *target_attn, thin[18], thin[19],
        *cross_attn, thin[16], thin[17],
        target_wide[0], bias(9), target_wide[1], thin[13], thin[14], thin[15],
    )


def solution(mesh):
    rows = P("dp", "pipe", None)
    matrix, vector = P("dp", None), P("dp")
    in_specs = (rows, rows, P("dp"), P("dp"), rows, rows) + (P(),) * 27
    attention = (matrix, matrix, matrix, vector, vector)
    ffn = (matrix, vector, matrix, vector, vector, vector)
    out_specs = (rows,) * 4 + attention + ffn + attention + attention + ffn
    return jax.shard_map(shards, mesh=mesh, in_specs=in_specs, out_specs=out_specs, check_vma=False)
```

```python
import functools

import jax
import jax.numpy as jnp
from jax import lax
from jax.experimental import pallas as pl
from jax.experimental.pallas import tpu as pltpu
from jax.sharding import PartitionSpec as P

HEAD_DIM = 64
PAIR = 2 * HEAD_DIM
LOG2E = 1.4426950408889634
LN2 = 0.6931471805599453
HIDDEN = -1e30
BF = jnp.bfloat16
F32 = jnp.float32
VMEM_BYTES = 56 * 2**20
SMALL_BYTES = 16 * 2**20


def product(left, right, sides):
    return lax.dot_general(left, right, (sides, ((), ())), preferred_element_type=F32)


def nn(left, right):
    return product(left, right, ((1,), (0,)))


def nt(left, right):
    return product(left, right, ((1,), (1,)))


def tn(left, right):
    return product(left, right, ((0,), (0,)))


def norm_forward(value):
    center = value - jnp.mean(value, -1, keepdims=True)
    inverse = lax.rsqrt(jnp.mean(center * center, -1, keepdims=True) + 1e-05)
    return center * inverse, inverse


def norm_backward(gradient, normed, inverse, gain):
    scaled = gradient * gain
    back = inverse * (
        scaled
        - jnp.mean(scaled, -1, keepdims=True)
        - normed * jnp.mean(scaled * normed, -1, keepdims=True)
    )
    return (
        back,
        jnp.sum(gradient * normed, 0, keepdims=True),
        jnp.sum(gradient, 0, keepdims=True),
    )


def fill_bias(place_ref, count, causal, bias_ref):
    keys, width = bias_ref.shape
    rows = keys // 4
    for block in range(4):
        first = block * rows if causal else place_ref[block]
        at = first + lax.broadcasted_iota(jnp.int32, (rows, width), 0)
        allowed = at < count
        if causal:
            lane = lax.broadcasted_iota(jnp.int32, (rows, width), 1)
            asked = jnp.where(lane < rows, place_ref[0] + lane, place_ref[1] + lane - rows)
            allowed = allowed & (at <= asked)
        bias_ref[block * rows : (block + 1) * rows, :] = jnp.where(allowed, 0.0, HIDDEN)


def by_core(place_ref, rows, keys, run):
    block = rows // 2
    for core in range(2):
        seen = (core + 1, keys // block - core)

        @pl.when(place_ref[6] == core)
        def _(seen=seen):
            run(tuple((at * block, (at + 1) * block, count * block) for at, count in enumerate(seen)))


def bias_of(bias_ref, first, last, keys):
    width = bias_ref.shape[1]
    if width > 128:
        return bias_ref[:keys, first:last]
    return jnp.concatenate([bias_ref[:keys, :]] * ((last - first) // width), 1)


def head_lanes(half):
    lane = lax.broadcasted_iota(jnp.int32, (1, PAIR), 1)
    return (lane >= HEAD_DIM * half) & (lane < HEAD_DIM * (half + 1))


def project(own, other_ref, wq, wkv, q_ref, k_ref, v_ref, own_keys=None, starts=None):
    rows, width = own.shape
    q_ref[...] = (nn(own, wq[...]) * (HEAD_DIM**-0.5 * LOG2E)).astype(BF)
    keys = own if own_keys is None else own_keys
    for at in (0, rows):
        for ref, part in ((k_ref, wkv[:, :width]), (v_ref, wkv[:, width:])):
            value = nn(keys, part).astype(BF)
            if starts is None:
                ref[at : at + rows, :] = value
                continue
            block = rows // 2
            for half in range(2):
                first = pl.multiple_of(starts[2 * at // rows + half], block)
                ref[pl.ds(first, block), :] = value[half * block : (half + 1) * block]
        keys = other_ref[...]


def attend(spans, step, q_ref, k_ref, v_ref, bias_ref, ot_ref, lse_ref):
    def one_head(index, half):
        cols = pl.ds(pl.multiple_of(index // 2 * PAIR, PAIR), PAIR)
        at = pl.multiple_of(index * HEAD_DIM, HEAD_DIM)
        values = v_ref[:, cols].T
        if isinstance(half, int):
            values = values[HEAD_DIM * half : HEAD_DIM * (half + 1)]
        else:
            values = jnp.where(half == 0, values[:HEAD_DIM], values[HEAD_DIM:])
        for first, last, seen in spans:
            queries, keys = q_ref[first:last, cols], k_ref[:seen, cols]
            masked = jnp.where(head_lanes(half), queries, jnp.zeros_like(queries))
            scores = nt(keys, masked) + bias_of(bias_ref, first, last, seen)
            top = jnp.max(scores, 0, keepdims=True)
            expon = jnp.exp2(scores - top)
            total = jnp.sum(expon, 0, keepdims=True)
            mixed = nn(values[:, :seen], expon.astype(BF))
            ot_ref[pl.ds(at, HEAD_DIM), first:last] = mixed / total
            lse_ref[pl.ds(index, 1), first:last] = top + jnp.log2(total)

    def heads(index, carry):
        for half in range(step):
            one_head(step * index + half, half if step == 2 else index % 2)
        return carry

    lax.fori_loop(0, q_ref.shape[1] // HEAD_DIM // step, heads, 0)


def attend_back(
    spans, q_ref, k_ref, v_ref, do_ref, bias_ref, lse_ref, delta_ref, dqt_ref, dk_ref, dv_ref
):
    def pair(index, carry):
        cols = pl.ds(pl.multiple_of(index * PAIR, PAIR), PAIR)
        turned = k_ref[:, cols].T
        done = 0
        for first, last, seen in spans:
            keys, values = k_ref[:seen, cols], v_ref[:seen, cols]
            queries, grads = q_ref[first:last, cols], do_ref[first:last, cols]
            dkeys = dvalues = None
            for half in range(2):
                mine = head_lanes(half)
                masked = jnp.where(mine, queries, jnp.zeros_like(queries))
                masked_grads = jnp.where(mine, grads, jnp.zeros_like(grads))
                head = pl.ds(2 * index + half, 1)
                scores = nt(keys, masked) + bias_of(bias_ref, first, last, seen)
                probs = jnp.exp2(scores - lse_ref[head, first:last])
                dprobs = nt(values, masked_grads)
                dscores = (probs * (dprobs - delta_ref[head, first:last])).astype(BF)
                part = nn(probs.astype(BF), masked_grads)
                dvalues = part if half == 0 else dvalues + part
                part = nn(dscores, masked)
                dkeys = part if half == 0 else dkeys + part
                dquery = nn(turned[HEAD_DIM * half : HEAD_DIM * (half + 1), :seen], dscores)
                at = pl.multiple_of(index * PAIR + HEAD_DIM * half, HEAD_DIM)
                dqt_ref[pl.ds(at, HEAD_DIM), first:last] = (dquery * HEAD_DIM**-0.5).astype(BF)
            dkeys = dkeys * LN2
            if done:
                dkeys = jnp.concatenate([dkeys[:done] + dk_ref[:done, cols].astype(F32), dkeys[done:]], 0)
                dvalues = jnp.concatenate([dvalues[:done] + dv_ref[:done, cols].astype(F32), dvalues[done:]], 0)
            dk_ref[:seen, cols] = dkeys.astype(BF)
            dv_ref[:seen, cols] = dvalues.astype(BF)
            done = seen
        if done < k_ref.shape[0]:
            rest = jnp.zeros((k_ref.shape[0] - done, PAIR), BF)
            dk_ref[done:, cols] = rest
            dv_ref[done:, cols] = rest
        return carry

    lax.fori_loop(0, q_ref.shape[1] // PAIR, pair, 0)


class Spread:
    def __init__(self, core, keep_ref, send_ref):
        self.first = core == 0
        self.keep_ref, self.send_ref = keep_ref, send_ref
        self.quarters, self.planes, self.rows = keep_ref.shape[:3]

    def put(self, quarter, plane, at, even, odd):
        even, odd = even.astype(BF), odd.astype(BF)
        rows = slice(at, at + even.shape[0])
        self.keep_ref[quarter, plane, rows, :] = jnp.where(self.first, even, odd)
        self.send_ref[quarter, plane, rows, :] = jnp.where(self.first, odd, even)

    def square(self, value, at):
        chunk = value.shape[0] // (2 * self.planes)
        piece = chunk // self.quarters
        for plane in range(self.planes):
            for quarter in range(self.quarters):
                even = 2 * plane * chunk + quarter * piece
                odd = even + chunk
                self.put(quarter, plane, at, value[even : even + piece], value[odd : odd + piece])

    def columns(self, value, quarter, at):
        chunk = value.shape[0] // (2 * self.planes)
        for plane in range(self.planes):
            even = 2 * plane * chunk
            odd = even + chunk
            self.put(quarter, plane, at, value[even : even + chunk], value[odd : odd + chunk])

    def two_chunks(self, value, plane, at):
        chunk = value.shape[0] // 2
        piece = chunk // self.quarters
        for quarter in range(self.quarters):
            even = quarter * piece
            odd = even + chunk
            self.put(quarter, plane, at, value[even : even + piece], value[odd : odd + piece])

    def same(self, quarter, at, value):
        for plane in range(self.planes):
            self.put(quarter, plane, at, value, value)


class Chunks(Spread):
    def __init__(self, ref):
        self.ref = ref
        self.quarters, self.planes, self.rows = ref.shape[1], ref.shape[0] // 2, ref.shape[2]

    def put(self, quarter, plane, at, even, odd):
        rows = slice(at, at + even.shape[0])
        self.ref[2 * plane, quarter, rows, :] = even.astype(BF)
        self.ref[2 * plane + 1, quarter, rows, :] = odd.astype(BF)


class Whole:
    def __init__(self, refs):
        self.refs = refs


def spread_of(io, refs):
    if isinstance(refs, list) and len(refs) == 2:
        return Spread(io.place[6], *refs)
    if isinstance(refs, list):
        return Whole(refs)
    return Chunks(refs)


def spread_attention(spread, own, keys_own, keys_other, dar, ot_ref, dqt_ref, dk, dv):
    rows, width = dar.shape
    dq = dqt_ref[...].T
    own_t = own[...].T
    keys_t = own_t if keys_own is own else keys_own[...].T
    other_t = keys_other[...].T
    dwo = nn(ot_ref[...].astype(BF), dar)
    dwq = nn(own_t, dq)
    dwk = nn(keys_t, dk[0]) + nn(other_t, dk[1])
    dwv = nn(keys_t, dv[0]) + nn(other_t, dv[1])
    if isinstance(spread, Whole):
        wq_ref, wkv_ref, wo_ref = spread.refs
        wq_ref[...] = dwq.astype(BF)
        wkv_ref[:, :width] = dwk.astype(BF)
        wkv_ref[:, width:] = dwv.astype(BF)
        wo_ref[...] = dwo.astype(BF)
        return
    piece = spread.rows // 4
    for place, value in enumerate((dwq, dwk, dwv, dwo)):
        spread.square(value, place * piece)


BLOCK = 512
TANH_SCALE = 0.7978845608028654
TANH_CUBE = 0.044715


def expand(hidden, w1, b1, active_ref, slope_ref):
    for at in range(0, w1.shape[1], BLOCK):
        cols = slice(at, at + BLOCK)
        before = nn(hidden, w1[:, cols]) + b1[:, cols]
        square = before * before
        inner = before * (TANH_SCALE + (TANH_SCALE * TANH_CUBE) * square)
        curve = jnp.tanh(inner)
        half = 0.5 * (1.0 + curve)
        active_ref[:, cols] = (before * half).astype(BF)
        steep = TANH_SCALE + (3 * TANH_SCALE * TANH_CUBE) * square
        slope_ref[:, cols] = (half + (0.5 * before) * (1.0 - curve * curve) * steep).astype(BF)


def contract(hidden, residual, active_ref, w2, b2):
    total = hidden.astype(F32) + nn(active_ref[...], w2[...]) + b2[...] + residual.astype(F32)
    return norm_forward(total)


def ffn_backward(io, spread, back, hidden, parts, bias_grad_ref):
    low = back.astype(BF)
    hidden_t = hidden.T
    dhidden = None
    for number in range(bias_grad_ref.shape[0]):
        w1, w2, active, slope = parts(number)
        dactive = nt(low, w2).astype(BF)
        dbefore = (dactive.astype(F32) * slope.astype(F32)).astype(BF)
        bias_grad_ref[number : number + 1, :] = jnp.sum(dbefore.astype(F32), 0, keepdims=True)
        dcontract = tn(active, low)
        dexpand = nn(hidden_t, dbefore)
        if isinstance(spread, Whole):
            block = slice(number * BLOCK, (number + 1) * BLOCK)
            spread.refs[0][:, block] = dexpand.astype(BF)
            spread.refs[1][block, :] = dcontract.astype(BF)
        else:
            chunk = dexpand.shape[0] // (2 * spread.planes)
            spread.columns(dexpand, number, 0)
            spread.two_chunks(dcontract, number, chunk)
            io.send_part(spread.ref, 2 * number, (slice(None), number, slice(0, chunk)))
            pair = slice(2 * number, 2 * number + 2)
            io.send_part(spread.ref, 2 * number + 1, (pair, slice(None), slice(chunk, 2 * chunk)))
        part = nt(dbefore, w1)
        dhidden = part if dhidden is None else dhidden + part
    return dhidden, jnp.sum(low.astype(F32), 0, keepdims=True)


PARTS = 12


class Buffers:
    def __init__(self, place, ins, outs, small):
        self.place, self.ins, self.outs, self.small = place, ins, outs, small
        self.waiting, self.going = {}, []
        self.queue, late = [], []
        for name, entry in ins.items():
            if entry is None:
                self.ahead()
                continue
            buffer, sources, sems = entry
            copies = [
                pltpu.make_async_copy(source, buffer.at[where], sems.at[number])
                for number, (source, where) in enumerate(sources)
            ]
            self.waiting[name] = copies
            if len(copies) > 2:
                late.append(copies)
            else:
                self.queue += copies
        for copies in zip(*late, strict=True):
            self.queue += copies
        if None not in ins.values():
            self.ahead()
        self.sent = set()

    def __getattr__(self, name):
        if name in self.small:
            return self.small[name]
        if name in self.outs:
            buffers = self.outs[name]
            return [buffer for buffer, _, _ in buffers] if isinstance(buffers, list) else buffers[0]
        for copy in self.waiting[name]:
            self.wait(copy)
        self.waiting[name] = []
        return self.ins[name][0]

    def block(self, name, number):
        self.wait(self.waiting[name][number])
        if number + 1 == len(self.waiting[name]):
            self.waiting[name] = []
        return self.ins[name][0]

    def ahead(self):
        for copy in self.queue:
            copy.start()
        self.queue = []

    def wait(self, copy):
        if any(copy is other for other in self.queue):
            self.ahead()
        copy.wait()

    def results(self):
        for entry in self.outs.values():
            yield from entry if isinstance(entry, list) else [entry]

    def start(self, copy):
        copy.start()
        self.going.append(copy)

    def send(self, *refs):
        for buffer, targets, sems in self.results():
            if any(buffer is ref for ref in refs):
                self.sent.add(id(buffer))
                for number, (target, where) in enumerate(targets):
                    self.start(pltpu.make_async_copy(buffer.at[where], target, sems.at[number]))

    def send_part(self, ref, number, where):
        for buffer, targets, sems in self.results():
            if buffer is ref:
                self.sent.add(id(buffer))
                self.start(
                    pltpu.make_async_copy(buffer.at[where], targets[0][0].at[where], sems.at[number])
                )

    def finish(self):
        self.send(*[entry[0] for entry in self.results() if id(entry[0]) not in self.sent])
        for copies in self.waiting.values():
            for copy in copies:
                self.wait(copy)
        for copy in self.going:
            copy.wait()


class Part:
    def __init__(self, io, prefix):
        self.io, self.prefix = io, prefix
        self.place, self.send, self.ahead = io.place, io.send, io.ahead

    def __getattr__(self, name):
        return getattr(self.io, self.prefix + name)


class Ends(list):
    pass


class Blocks:
    def __init__(self, array, axis):
        self.array, self.axis = array, axis


def run(kernel, name, flops, place, ins, small, outs, scratch=(), vmem_bytes=VMEM_BYTES):
    arrays, buffers, sem_counts, shapes = [], [], [], []
    in_plan, out_plan = {}, {}

    def buffer(dims, dtype, sems):
        buffers.append(pltpu.VMEM(tuple(dims), dtype))
        sem_counts.append(sems)
        return len(buffers) - 1

    for key, value in ins.items():
        if value is None:
            in_plan[key] = None
            continue
        plan = []
        if isinstance(value, Blocks):
            array, axis = value.array, value.axis
            for at in range(0, array.shape[axis], BLOCK):
                where = (slice(None),) * axis + (slice(at, at + BLOCK),)
                plan.append((len(arrays), where, where))
            arrays.append(array)
            dims, dtype = array.shape, array.dtype
        else:
            rows = 0
            for part in value if isinstance(value, Ends) else [value]:
                array, index = part if isinstance(part, tuple) else (part, None)
                dims = array.shape if index is None else array.shape[1:]
                where = len(plan) if isinstance(value, Ends) else ()
                plan.append((len(arrays), () if index is None else (index,), where))
                rows += dims[0]
                arrays.append(array)
            dims, dtype = (rows, *dims[1:]), array.dtype
        in_plan[key] = (buffer(dims, dtype, len(plan)), plan)

    def plan_out(value):
        if isinstance(value, Ends):
            plan = [(len(shapes) + number, number) for number in range(len(value))]
            shapes.extend(value)
            rows = sum(part.shape[0] for part in value)
            return buffer((rows, *value[0].shape[1:]), value[0].dtype, len(plan)), plan
        shapes.append(value)
        return buffer(value.shape, value.dtype, PARTS), [(len(shapes) - 1, ())]

    for key, value in outs.items():
        whole = isinstance(value, list) and not isinstance(value, Ends)
        out_plan[key] = [plan_out(part) for part in value] if whole else plan_out(value)

    def body(place_ref, *refs):
        cuts = (len(small), len(arrays), len(shapes), len(buffers), len(sem_counts))
        groups, at = [], 0
        for count in cuts:
            groups.append(refs[at : at + count])
            at += count
        small_refs, in_refs, out_refs, buffer_refs, sems = groups

        def part_of(ref, where):
            return ref.at[where] if where else ref

        def settled(where, rows):
            if not isinstance(where, int):
                return where
            return (pl.ds(pl.multiple_of((place_ref[9] ^ where) * rows, rows), rows),)

        def out_entry(plan):
            number, targets = plan
            return (
                buffer_refs[number],
                [(out_refs[which], settled(where, out_refs[which].shape[0])) for which, where in targets],
                sems[number],
            )

        def in_entry(number, plan):
            parts = []
            for which, where, to in plan:
                source = part_of(in_refs[which], where)
                parts.append((source, settled(to, source.shape[0])))
            return buffer_refs[number], parts, sems[number]

        in_map = {key: plan and in_entry(*plan) for key, plan in in_plan.items()}
        out_map = {
            key: [out_entry(part) for part in plan] if isinstance(plan, list) else out_entry(plan)
            for key, plan in out_plan.items()
        }
        io = Buffers(place_ref, in_map, out_map, dict(zip(small, small_refs, strict=True)))
        kernel(io, *refs[at:])
        io.finish()

    vmem, anywhere = pl.BlockSpec(memory_space=pltpu.VMEM), pl.BlockSpec(memory_space=pl.ANY)
    moved = sum(a.size * a.dtype.itemsize for a in (*arrays, *shapes))
    results = pl.pallas_call(
        body,
        out_shape=shapes,
        in_specs=[pl.BlockSpec(memory_space=pltpu.SMEM)] + [vmem] * len(small) + [anywhere] * len(arrays),
        out_specs=[anywhere] * len(shapes),
        scratch_shapes=[*buffers, *[pltpu.SemaphoreType.DMA((count,)) for count in sem_counts], *scratch],
        name=name,
        cost_estimate=pl.CostEstimate(flops=flops, bytes_accessed=moved, transcendentals=0),
        compiler_params=pltpu.CompilerParams(vmem_limit_bytes=vmem_bytes),
    )(place, *small.values(), *arrays)

    def named(plan):
        if isinstance(plan, list):
            return [named(part) for part in plan]
        got = [results[which] for which, _ in plan[1]]
        return got if len(got) > 1 else got[0]

    return Results({key: named(plan) for key, plan in out_plan.items()})


class Results(dict):
    def __getattr__(self, name):
        return self[name]


def put_norm(io, normed, inverse, normed_ref, inverse_ref):
    normed_ref[...] = normed
    inverse_ref[...] = jnp.broadcast_to(inverse, inverse_ref.shape)
    io.send(normed_ref, inverse_ref)


def self_attention(io, count_at, causal, bias_ref):
    fill_bias(io.place, io.place[count_at], causal, bias_ref)
    rows = io.own[...]
    starts = [io.place[block] for block in range(4)] if causal else None
    project(rows, io.other, io.wq, io.wkv, io.q, io.k, io.v, starts=starts)
    io.send(io.q, io.k, io.v)
    io.ahead()
    q, k, v, ot, lse = io.q, io.k, io.v, io.ot, io.lse
    whole = ((0, q.shape[0], k.shape[0]),)
    attend(whole, 2, q, k, v, bias_ref, ot, lse)
    io.send(ot, lse)
    return tn(ot[...].astype(BF), io.wo[...]), rows


def run_spans(io, causal, run):
    rows, keys = io.q.shape[0], io.k.shape[0]
    if causal:
        by_core(io.place, rows, keys, run)
    else:
        run(((0, rows, keys),))


def encoder_forward_kernel(io, bias_ref):
    attn, rows = self_attention(io, 4, False, bias_ref)
    normed, inverse = norm_forward(rows.astype(F32) + attn)
    put_norm(io, normed, inverse, io.n0, io.i0)
    hidden = (normed * io.gain[...] + io.offset[...]).astype(BF)
    io.hidden[...] = hidden
    io.send(io.hidden)
    expand(hidden, io.w1, io.b1, io.active, io.slope)
    io.send(io.active, io.slope)
    normed, inverse = contract(hidden, rows, io.active, io.w2, io.b2)
    io.memory[...] = (normed * io.scale[...] + io.center[...]).astype(BF)
    io.send(io.memory)
    put_norm(io, normed, inverse, io.n1, io.i1)


def decoder_forward_kernel(io, causal_ref, bias_ref, active_ref, slope_ref):
    attn, rows = self_attention(Part(io, "s"), 5, True, causal_ref)
    normed, inverse = norm_forward(rows.astype(F32) + attn)
    put_norm(io, normed, inverse, io.n, io.i)
    spread = spread_of(io, io.grads)
    fill_bias(io.place, io.place[4], False, bias_ref)
    first = io.n[...] * io.gain[...] + io.offset[...]
    first_low = first.astype(BF)
    io.first[...] = first_low
    io.send(io.first)
    memory = io.mem_own[...]
    project(first_low, io.mem_other, io.wq, io.wkv, io.q, io.k, io.v, memory)
    io.send(io.q, io.k, io.v)
    io.ahead()
    q, k, v, ot, lse = io.q, io.k, io.v, io.ot, io.lse
    whole = ((0, q.shape[0], k.shape[0]),)
    attend(whole, 2, q, k, v, bias_ref, ot, lse)
    io.send(io.ot, io.lse)
    n2, i2 = norm_forward(first + tn(io.ot[...].astype(BF), io.wo[...]))
    second = (n2 * io.cross_gain[...] + io.cross_offset[...]).astype(BF)
    expand(second, io.w1, io.b1, active_ref, slope_ref)
    n3, i3 = contract(second, io.sown[...], active_ref, io.w2, io.b2)
    output = (n3 * io.scale[...] + io.center[...]).astype(BF)
    block = output.shape[0] // 2
    for half in range(2):
        rows = slice(half * block, (half + 1) * block)
        io.result[2 * half] = memory[rows]
        io.result[2 * half + 1] = output[rows]
    io.send(io.result)
    back, dscale, dcenter = norm_backward(io.cotangent[...].astype(F32), n3, i3, io.scale[...])
    io.dr[...] = back
    io.send(io.dr)
    w1, w2 = io.w1, io.w2

    def parts(number):
        cut = slice(number * BLOCK, (number + 1) * BLOCK)
        return w1[:, cut], w2[cut, :], active_ref[:, cut], slope_ref[:, cut]

    vecs = io.vecs
    dhidden, dshift = ffn_backward(io, spread, back, second, parts, vecs.at[0:4])
    dsecond = (back + dhidden).astype(BF).astype(F32)
    dv2, dgain, doffset = norm_backward(dsecond, n2, i2, io.cross_gain[...])
    io.dv[...] = dv2
    io.send(io.dv)
    put_rows(vecs, 4, (dshift, dscale, dcenter, dgain, doffset))


def put_rows(ref, at, values):
    for row, value in enumerate(values):
        ref[at + row : at + row + 1, :] = value
    at += len(values)
    ref[at:, :] = jnp.zeros((ref.shape[0] - at, ref.shape[1]), F32)


def cross_backward_kernel(io, bias_ref, *scratch):
    fill_bias(io.place, io.place[4], False, bias_ref)
    dv2 = io.dv[...]
    du, dc_own, dc_other = attention_backward(
        io, False, bias_ref, scratch, dv2.astype(BF), "first", "mem_own", "mem_other"
    )
    io.dmem_other[...] = dc_other.astype(BF)
    io.dmem_own[...] = dc_own.astype(BF)
    io.send(io.dmem_other, io.dmem_own)
    dv1, dgain, doffset = norm_backward(dv2 + du, io.n[...], io.i[:, :1], io.gain[...])
    io.dv1[...] = dv1
    io.send(io.dv1)
    put_rows(io.vecs, 0, (dgain, doffset))


def self_backward(io, count_at, causal, bias_ref, scratch):
    fill_bias(io.place, io.place[count_at], causal, bias_ref)
    dv = io.dv[...]
    du, dc_own, dc_other = attention_backward(
        io, causal, bias_ref, scratch, dv.astype(BF), "own", "own", "other"
    )
    io.dc_other[...] = dc_other.astype(BF)
    io.send(io.dc_other)
    io.du[...] = (dv + io.extra[...] + du + dc_own).astype(BF)
    io.send(io.du)


def source_backward_kernel(io, bias_ref, *scratch):
    self_backward(io, 4, False, bias_ref, scratch)


def target_backward_kernel(io, bias_ref, *scratch):
    self_backward(io, 5, True, bias_ref, scratch)


def attention_backward(io, causal, bias_ref, scratch, dar, own, keys_own, keys_other):
    spread = spread_of(io, io.grads)
    do_ref, delta_ref, dqt_ref, dk_ref, dv_ref = scratch
    rows, width = dar.shape
    wo, ot = io.wo, io.ot
    do_ref[...] = nt(dar, wo[...]).astype(BF)
    turned = nt(wo[...], dar).astype(BF).astype(F32) * ot[...]
    delta_ref[...] = jnp.sum(turned.reshape(width // HEAD_DIM, HEAD_DIM, rows), 1)
    queries, keys, values, lse = io.q, io.k, io.v, io.lse
    io.ahead()
    run_spans(
        io,
        causal,
        lambda spans: attend_back(
            spans, queries, keys, values, do_ref, bias_ref, lse, delta_ref, dqt_ref, dk_ref, dv_ref
        ),
    )
    if causal:
        starts = [io.place[block] for block in range(4)]
        dk, dv = [
            [
                jnp.concatenate([ref[pl.ds(pl.multiple_of(first, rows // 2), rows // 2), :] for first in firsts], 0)
                for firsts in (starts[:2], starts[2:])
            ]
            for ref in (dk_ref, dv_ref)
        ]
    else:
        dk, dv = [[ref[:rows, :], ref[rows:, :]] for ref in (dk_ref, dv_ref)]
    own_ref = getattr(io, own)
    keys_ref = own_ref if keys_own == own else getattr(io, keys_own)
    spread_attention(spread, own_ref, keys_ref, getattr(io, keys_other), dar, ot, dqt_ref, dk, dv)
    io.send(*io.grads)
    dq = dqt_ref[...].T
    wkv = io.wkv
    dc = [
        nt(dk[at], wkv[:, :width]) + nt(dv[at], wkv[:, width:])
        for at in (1, 0)
    ]
    return nt(dq, io.wq[...]), dc[1], dc[0]


def encoder_ffn_backward(io):
    spread = spread_of(io, io.grads)
    dmemory = (io.dmem_own[...].astype(F32) + io.dmem_came[...].astype(F32)).astype(BF).astype(F32)
    total = io.cotangent[...].astype(F32) + dmemory
    back, dscale, dcenter = norm_backward(total, io.n1[...], io.i1[:, :1], io.scale[...])
    io.dr[...] = back
    io.send(io.dr)

    def parts(number):
        cut = slice(number * BLOCK, (number + 1) * BLOCK)
        return (
            io.block("w1", number)[:, cut],
            io.block("w2", number)[cut, :],
            io.block("active", number)[:, cut],
            io.block("slope", number)[:, cut],
        )

    vecs = io.vecs
    dhidden, dshift = ffn_backward(io, spread, back, io.hidden[...], parts, vecs.at[0:4])
    dlow = (back + dhidden).astype(BF).astype(F32)
    dv0, dgain, doffset = norm_backward(dlow, io.n0[...], io.i0[:, :1], io.gain[...])
    io.dv[...] = dv0
    io.send(io.dv)
    top, cross = io.top_vecs, io.cross_vecs
    rest = [top[row : row + 1, :] for row in range(9)] + [cross[row : row + 1, :] for row in range(2)]
    put_rows(vecs, 4, (dshift, dscale, dcenter, dgain, doffset, *rest))
    if not isinstance(spread, Whole):
        share = vecs.shape[0] // spread.quarters
        for quarter in range(spread.quarters):
            spread.same(quarter, spread.rows - share, vecs[quarter * share : (quarter + 1) * share, :])
        where = (slice(None), slice(None), slice(spread.rows - share, spread.rows))
        io.send_part(spread.ref, PARTS - 1, where)


def small_kernel(body, name, outs, place, *args):
    vmem = pl.BlockSpec(memory_space=pltpu.VMEM)
    moved = sum(a.size * a.dtype.itemsize for a in (*args, *outs))
    return pl.pallas_call(
        body,
        out_shape=outs,
        in_specs=[pl.BlockSpec(memory_space=pltpu.SMEM)] + [vmem] * len(args),
        out_specs=[vmem] * len(outs),
        name=name,
        cost_estimate=pl.CostEstimate(flops=0, bytes_accessed=moved, transcendentals=0),
        compiler_params=pltpu.CompilerParams(vmem_limit_bytes=SMALL_BYTES),
    )(place, *args)


def split_kernel(pairs, extra, place_ref, *refs):
    outs = refs[2 * pairs + extra :]
    for step, out_ref in enumerate(outs):
        quarter = place_ref[7] ^ step
        at = 0
        for plane in range(refs[0].shape[1]):
            for pair in range(pairs):
                keep_ref, came_ref = refs[2 * pair : 2 * pair + 2]
                rows = keep_ref.shape[2]
                total = keep_ref[quarter, plane].astype(F32) + came_ref[quarter, plane].astype(F32)
                out_ref[at : at + rows, :] = total.astype(BF)
                at += rows
        if extra:
            out_ref[at:, :] = refs[2 * pairs][quarter]


def split_pieces(place, pairs, extra=None):
    quarters, planes, _, width = pairs[0][0].shape
    rows = planes * sum(keep.shape[2] for keep, _ in pairs)
    args = [part for pair in pairs for part in pair]
    if extra is not None:
        rows += extra.shape[1]
        args.append(extra)
    body = functools.partial(split_kernel, len(pairs), int(extra is not None))
    outs = [jax.ShapeDtypeStruct((rows, width), BF)] * quarters
    return list(small_kernel(body, "split", outs, place, *args))


def join_kernel(place_ref, whole_ref, pieces_ref, *outs):
    rows = whole_ref.shape[0]
    for step, out_ref in enumerate(outs):
        out_ref[:rows, :] = whole_ref[...]
        out_ref[rows:, :] = pieces_ref[place_ref[7] ^ step]


def join_pieces(place, whole, pieces):
    outs = [jax.ShapeDtypeStruct((whole.shape[0] + pieces.shape[1], whole.shape[1]), BF)] * pieces.shape[0]
    return list(small_kernel(join_kernel, "join", outs, place, whole, pieces))


def home_kernel(place_ref, *refs):
    dus, came_refs, outs = (refs[:2], refs[2:4]), refs[4:6], refs[6:]
    rows = outs[0].shape[1]
    for which, out_ref in enumerate(outs):
        at = pl.multiple_of((place_ref[9] ^ which) * rows, rows)
        for number, (du, came_ref) in enumerate(zip(dus, came_refs, strict=True)):
            out_ref[number] = (du[which][...].astype(F32) + came_ref[pl.ds(at, rows), :].astype(F32)).astype(BF)


def home_blocks(place, source_du, source_came, target_du, target_came):
    outs = [jax.ShapeDtypeStruct((2, *source_du[0].shape), BF)] * 2
    return list(small_kernel(home_kernel, "home", outs, place, *source_du, *target_du, source_came, target_came))


def fold_kernel(sets, planes, with_ready, place_ref, *refs):
    parts, outs = refs[:-planes], refs[-planes:]
    above = 0
    if with_ready:
        ready, parts = parts[-planes:], parts[:-planes]
        above = ready[0].shape[0]
    quarters, rows = len(parts) // sets, (outs[0].shape[0] - above) // sets
    for step, out_ref in enumerate(outs):
        if with_ready:
            out_ref[:above, :] = ready[step][...]
        plane = (place_ref[8] // 2) ^ step
        where = pl.ds(pl.multiple_of(plane * rows, rows), rows)
        for number in range(sets):
            of_set = parts[number * quarters : (number + 1) * quarters]
            total = sum(part[where, :].astype(F32) for part in of_set)
            at = above + number * rows
            out_ref[at : at + rows, :] = total.astype(BF)


def fold_pieces(place, sets, planes, height, ready=()):
    rows = len(sets) * height // planes + (ready[0].shape[0] if ready else 0)
    outs = [jax.ShapeDtypeStruct((rows, sets[0][0].shape[1]), BF)] * planes
    body = functools.partial(fold_kernel, len(sets), planes, bool(ready))
    return list(small_kernel(body, "fold", outs, place, *[part for parts in sets for part in parts], *ready))


def unpack_kernel(plan, io):
    chip, group = io.place[7], io.place[8]
    pieces = [ref for key, ref in io.small.items()]
    if len(pieces) == 1:
        pieces = [(quarter, pieces[0].at[quarter]) for quarter in range(pieces[0].shape[0])]
    else:
        pieces = [(chip ^ step, ref) for step, ref in enumerate(pieces)]
    quarters = len(pieces)
    for quarter, piece_ref in pieces:
        width = piece_ref.shape[1]
        at = 0
        for kind, outs in plan:
            refs = getattr(io, outs)
            if kind == ATTENTION:
                size = refs[0].shape[0] // quarters
                rows = pl.ds(pl.multiple_of(quarter * size, size), size)
                values = [piece_ref[at + i * size : at + (i + 1) * size, :].astype(F32) for i in range(4)]
                refs[0][rows, :] = values[0]
                refs[1][rows, :width] = values[1]
                refs[1][rows, width:] = values[2]
                refs[2][rows, :] = values[3]
                at += 4 * size
            elif kind == FEEDFORWARD:
                size = refs[0].shape[0]
                cols = pl.ds(pl.multiple_of(quarter * width, width), width)
                refs[0][:, cols] = piece_ref[at : at + size, :].astype(F32)
                at += size
                size = refs[1].shape[0] // quarters
                rows = pl.ds(pl.multiple_of(quarter * size, size), size)
                refs[1][rows, :] = piece_ref[at : at + size, :].astype(F32)
                at += size
            else:
                size = piece_ref.shape[0] - at
                rows = pl.ds(pl.multiple_of(quarter * size, size), size)
                refs[0][rows, :] = piece_ref[at:, :].astype(F32)
    if kind == VECTORS:
        short = refs[1].shape[0]
        pair = refs[0][:, pl.ds(pl.multiple_of((group // 2) * 2 * short, 2 * short), 2 * short)]
        thin = jnp.where(group % 2 == 0, pair[:, :short], pair[:, short:])
        for number, at in enumerate(THIN_ROWS):
            refs[1 + number][...] = thin[at]
        long = 4 * short
        lanes = pl.ds(pl.multiple_of((group % 2) * long, long), long)
        for number, at in enumerate(LONG_ROWS):
            refs[1 + len(THIN_ROWS) + number][...] = refs[0][pl.ds(at + group // 2, 1), lanes][0]


ATTENTION, FEEDFORWARD, VECTORS = range(3)
THIN_ROWS = (4, 5, 6, 7, 8, 13, 14, 15, 16, 17, 18, 19)
LONG_ROWS = (0, 9)


class Places:
    def __init__(self, quarters, groups):
        self.quarters, self.groups = quarters, groups
        self.sends = []
        for which in range(2):
            pairs = []
            for quarter in range(quarters):
                for group in range(groups):
                    plane, core = divmod(group, 2)
                    worker = self.chip_of(core, self.place_of(quarter) ^ which)
                    target = worker * groups + 2 * plane + self.group_of(quarter)
                    pairs.append((quarter * groups + group, target))
            self.sends.append(pairs)
        self.cores = [(group, group ^ 1) for group in range(groups)]

    def group_of(self, quarter):
        return (quarter ^ (quarter >> 1)) & 1

    def place_of(self, quarter):
        return quarter >> 1

    def chip_of(self, group, place):
        return 2 * place + (group ^ place)

    def order(self, rows, upper):
        return [jnp.where(upper, rows[1], rows[0]), jnp.where(upper, rows[0], rows[1])]

    def to_work(self, parts):
        return [
            lax.ppermute(part, ("pipe", "dp"), pairs)
            for part, pairs in zip(parts, self.sends, strict=True)
        ]

    def to_home(self, block_a, block_b):
        return [
            lax.ppermute(part, ("pipe", "dp"), pairs)
            for part, pairs in zip((block_a, block_b), self.sends, strict=True)
        ]

    def at_home(self, came, upper):
        first, second = came
        return jnp.stack([jnp.where(upper, second, first), jnp.where(upper, first, second)])

    def to_other_core(self, value):
        return lax.ppermute(value, "dp", self.cores)


def gate(*values):
    return list(lax.optimization_barrier(values))


def together(*values):
    return lax.optimization_barrier(values)


def after(results, *flying):
    kept, flying = lax.optimization_barrier((dict(results), flying))
    return Results(kept), *flying


def to_quarters(parts):
    quarters = len(parts)
    return [
        part if step == 0 else lax.ppermute(part, "pipe", [(i, i ^ step) for i in range(quarters)])
        for step, part in enumerate(parts)
    ]


def to_planes(parts):
    groups = 2 * len(parts)
    return [
        part if step == 0 else lax.ppermute(part, "dp", [(i, i ^ (2 * step)) for i in range(groups)])
        for step, part in enumerate(parts)
    ]


def total_of(parts):
    return sum(part.astype(F32) for part in parts).astype(BF)


def by_step(value, index):
    return [
        lax.dynamic_index_in_dim(value, index ^ step, 0, keepdims=False) for step in range(value.shape[0])
    ]


def shards(
    source, target, source_length, target_length, memory_cotangent, output_cotangent,
    source_query, source_keyvalue, source_output, source_gain, source_offset,
    source_expand, source_bias, source_contract, source_shift, source_scale, source_center,
    target_query, target_keyvalue, target_output, target_gain, target_offset,
    cross_query, cross_keyvalue, cross_output, cross_gain, cross_offset,
    target_expand, target_bias, target_contract, target_shift, target_scale, target_center,
):
    quarters, groups = lax.axis_size("pipe"), lax.axis_size("dp")
    chip, group = lax.axis_index("pipe"), lax.axis_index("dp")
    core, planes = group % 2, groups // 2
    micro, block, width = source.shape
    rows, keys = 2 * block, 4 * block
    heads = width // HEAD_DIM
    wide = source_expand.shape[1]
    spread = (width // groups) % (16 * quarters) == 0
    places = Places(quarters, groups)
    upper = chip >= quarters // 2
    swap = places.to_other_core

    lengths = jnp.stack([source_length, target_length])
    other_lengths = swap(lengths)
    own = places.to_work(places.order(source, upper))
    counts = jnp.where(core == places.group_of(chip), lengths, other_lengths)
    counts = lax.dynamic_index_in_dim(counts, places.place_of(chip), 1, keepdims=False)
    starts = [places.chip_of(which, at) * block for which in (core, 1 - core) for at in range(2)]
    slots = [*starts, counts[0], counts[1], core, chip, group, places.place_of(chip)]
    place = jnp.stack([jnp.asarray(slot, jnp.int32) for slot in slots])
    late = places.order(jnp.stack([target, output_cotangent, memory_cotangent], 1), upper)
    own, late, place = together(own, late, place)
    other = Ends(swap(part) for part in own)
    own = Ends(own)
    late = places.to_work(late)


    def row(vector):
        return vector.reshape(1, -1)

    def shape(*dims, dtype=BF):
        return jax.ShapeDtypeStruct(dims, dtype)

    half = shape(block, width)
    sheet = shape(rows, width, dtype=F32)
    lanes = shape(rows, 128, dtype=F32)
    saved = Results(
        q=shape(rows, width), k=shape(keys, width), v=shape(keys, width),
        ot=shape(width, rows, dtype=F32), lse=shape(heads, rows, dtype=F32),
    )
    flat_bias = pltpu.VMEM((keys, 128), F32)
    causal_bias = pltpu.VMEM((keys, rows), F32)
    back_scratch = [
        pltpu.VMEM((rows, width), BF), pltpu.VMEM((heads, rows), F32), pltpu.VMEM((width, rows), BF),
        pltpu.VMEM((keys, width), BF), pltpu.VMEM((keys, width), BF),
    ]
    vec_rows = 16 * quarters
    if spread:
        attn_rows = 4 * width // (groups * quarters)
        ffn_rows = 2 * wide // (groups * quarters)
        attention_grads = [shape(quarters, planes, attn_rows, width)] * 2
        top_grads = shape(groups, quarters, ffn_rows, width)
        source_ffn_grads = shape(groups, quarters, ffn_rows + vec_rows // quarters, width)
    else:
        attention_grads = [shape(width, cols) for cols in (width, 2 * width, width)]
        top_grads = [shape(width, wide), shape(wide, width), shape(16, 128)]
        source_ffn_grads = top_grads
    core_flops = 2 * 4 * rows * keys * width
    linear_flops = 2 * rows * width * width
    ffn_flops = 4 * rows * width * wide
    attn_flops = 2 * core_flops + 8 * linear_flops
    attn_back_flops = 5 * core_flops + 16 * linear_flops

    encoder = run(
        encoder_forward_kernel, "encoder", attn_flops + ffn_flops, place,
        dict(own=own, wq=source_query, other=other, wkv=source_keyvalue, rest=None, wo=source_output, w1=source_expand,
             w2=source_contract),
        dict(gain=row(source_gain), offset=row(source_offset), b1=row(source_bias), b2=row(source_shift),
             scale=row(source_scale), center=row(source_center)),
        dict(**saved, n0=sheet, i0=lanes, hidden=shape(rows, width), active=shape(rows, wide),
             slope=shape(rows, wide), n1=sheet, i1=lanes, memory=shape(rows, width)),
        [flat_bias],
    )
    *late, memory = gate(*late, encoder.memory)
    target_own = Ends((part, 0) for part in late)
    target_other = Ends(swap(part[0]) for part in late)
    memory_other = swap(memory)
    top = run(
        decoder_forward_kernel, "decoder", 2 * attn_flops + 3 * ffn_flops, place,
        dict(sown=target_own, swq=target_query, sother=target_other, swkv=target_keyvalue, rest=None, swo=target_output,
             wq=cross_query, mem_own=memory, mem_other=memory_other, wkv=cross_keyvalue, wo=cross_output,
             w1=target_expand, w2=target_contract, cotangent=Ends((part, 1) for part in late)),
        dict(gain=row(target_gain), offset=row(target_offset), cross_gain=row(cross_gain),
             cross_offset=row(cross_offset), b1=row(target_bias), b2=row(target_shift), scale=row(target_scale),
             center=row(target_center)),
        dict(sq=saved.q, sk=saved.k, sv=saved.v, sot=saved.ot, slse=saved.lse, n=sheet, i=lanes, **saved,
             first=shape(rows, width), result=Ends([shape(2, block, width)] * 2), dr=sheet, dv=sheet,
             vecs=shape(16, width, dtype=F32), grads=top_grads),
        [causal_bias, flat_bias, pltpu.VMEM((rows, wide), BF), pltpu.VMEM((rows, wide), BF)],
    )
    results = places.to_home(*top.result)
    if spread:
        top_total = lax.psum_scatter(top.grads, "dp", scatter_dimension=0, tiled=True)[0]

    def kept(results):
        return dict(ot=results.ot, k=results.k, q=results.q, v=results.v, lse=results.lse, rest=None)

    decoder = Results(ot=top.sot, k=top.sk, q=top.sq, v=top.sv, lse=top.slse)

    cross = run(
        cross_backward_kernel, "cross_back", attn_back_flops, place,
        dict(dv=top.dv, wo=cross_output, **kept(top), first=top.first, mem_own=memory, mem_other=memory_other,
             wkv=cross_keyvalue, wq=cross_query, n=top.n, i=top.i),
        dict(gain=row(target_gain)),
        dict(dmem_own=shape(rows, width), dmem_other=shape(rows, width), dv1=sheet, vecs=shape(8, width, dtype=F32),
             grads=attention_grads),
        [flat_bias, *back_scratch],
    )
    cross, results = after(cross, results)
    results = places.at_home(results, upper)
    dmem_came = swap(cross.dmem_other)
    cross_came = swap(cross.grads[1]) if spread else ()
    target_back = run(
        target_backward_kernel, "target_back", attn_back_flops, place,
        dict(dv=cross.dv1, wo=target_output, **kept(decoder), own=target_own, other=target_other,
             wkv=target_keyvalue, wq=target_query, extra=top.dr),
        {}, dict(dc_other=shape(rows, width), du=Ends([half, half]), grads=attention_grads),
        [causal_bias, *back_scratch],
    )
    target_back, dmem_came, cross_came = after(target_back, dmem_came, cross_came)
    dtarget_came = swap(target_back.dc_other)
    target_came, early = (), ()
    if spread:
        target_came = swap(target_back.grads[1])
        early = split_pieces(place, [(cross.grads[0], cross_came)])
        early, dmem_came = together(early, dmem_came)
        early = to_quarters(early)
    source_ffn = run(
        encoder_ffn_backward, "source_ffn", 2 * ffn_flops, place,
        dict(cotangent=Ends((part, 2) for part in late), dmem_own=cross.dmem_own, dmem_came=dmem_came,
             n1=encoder.n1, i1=encoder.i1, w2=Blocks(source_contract, 0), slope=Blocks(encoder.slope, 1),
             w1=Blocks(source_expand, 1), active=Blocks(encoder.active, 1), hidden=encoder.hidden, n0=encoder.n0,
             i0=encoder.i0),
        dict(scale=row(source_scale), gain=row(source_gain), top_vecs=top.vecs, cross_vecs=cross.vecs),
        dict(dr=sheet, dv=sheet, vecs=shape(vec_rows, width, dtype=F32), grads=source_ffn_grads),
    )
    source_ffn, dtarget_came, target_came, early = after(source_ffn, dtarget_came, target_came, early)
    dv0, middle = source_ffn.dv, ()
    if spread:
        source_total = lax.psum_scatter(source_ffn.grads, "dp", scatter_dimension=0, tiled=True)[0]
        middle = split_pieces(place, [(target_back.grads[0], target_came)], top_total)
        dv0, middle = together(dv0, middle)
        middle = to_quarters(middle)
    source_back = run(
        source_backward_kernel, "source_back", attn_back_flops, place,
        dict(dv=dv0, wo=source_output, **kept(encoder), own=own, other=other, wkv=source_keyvalue,
             wq=source_query, extra=source_ffn.dr),
        {}, dict(dc_other=shape(rows, width), du=Ends([half, half]), grads=attention_grads),
        [flat_bias, *back_scratch],
    )
    source_back, middle = after(source_back, middle)

    def attention_outs():
        chunk = width // groups
        return [shape(chunk, width, dtype=F32), shape(chunk, 2 * width, dtype=F32), shape(chunk, width, dtype=F32)]

    def ffn_outs():
        return [shape(width // groups, wide, dtype=F32), shape(wide // groups, width, dtype=F32)]

    def unpack(name, plan, parts, outs):
        return run(
            functools.partial(unpack_kernel, plan), name, 0, place, {}, dict(enumerate(parts)), outs, vmem_bytes=SMALL_BYTES
        )

    dc_other = source_back.dc_other
    if spread:
        last_came = swap(source_back.grads[1])
        last = split_pieces(place, [(source_back.grads[0], last_came)])
        height = planes * attn_rows
        home = home_blocks(place, source_back.du, swap(dc_other), target_back.du, dtarget_came)
        last, home = together(last, home)
        last, home = to_quarters(last), places.to_home(*home)
        first = total_of([part[height:] for part in middle])
        ready = fold_pieces(place, [early, middle], planes, height)
        both = to_planes(fold_pieces(place, [last], planes, height, ready))
        pieces = to_quarters(join_pieces(place, first, source_total))
        both, pieces, home = together(both, pieces, home)
        first = pieces
        pieces = [part[ffn_rows:] for part in pieces]
        last = [jnp.concatenate([total_of(both), total_of(pieces)], 0)] * quarters
        last = to_quarters(last)
    else:
        home = home_blocks(place, source_back.du, swap(dc_other), target_back.du, dtarget_came)
        home = places.to_home(*home)
    gradients = places.at_home(home, upper).astype(F32)
    if spread:
        first_grads = unpack(
            "unpack_first", ((FEEDFORWARD, "top"),), first, dict(top=ffn_outs()),
        )
        last_grads = unpack(
            "unpack_last",
            (
                (ATTENTION, "cross"), (ATTENTION, "target"), (ATTENTION, "source"), (FEEDFORWARD, "low"),
                (VECTORS, "vectors"),
            ),
            last,
            dict(cross=attention_outs(), target=attention_outs(), source=attention_outs(), low=ffn_outs(),
                 vectors=[shape(vec_rows, width, dtype=F32)] + [shape(width // groups, dtype=F32)] * len(THIN_ROWS)
                 + [shape(wide // groups, dtype=F32)] * len(LONG_ROWS)),
        )
        thin = dict(zip(THIN_ROWS, last_grads.vectors[1:], strict=False))
        biases = dict(zip(LONG_ROWS, last_grads.vectors[-len(LONG_ROWS) :], strict=True))
        source_attn, target_attn, cross_attn = last_grads.source, last_grads.target, last_grads.cross
        source_wide, target_wide = last_grads.low, first_grads.top
    else:
        vectors = lax.psum(source_ffn.vecs, ("pipe", "dp"))
        thin = lax.dynamic_slice_in_dim(vectors, group * (width // groups), width // groups, 1)

        def reduced(parts):
            flat = jnp.concatenate([part.reshape(groups, -1) for part in parts], 1)
            total = lax.psum(lax.psum_scatter(flat, "dp", scatter_dimension=0, tiled=True)[0], "pipe")
            outs, at = [], 0
            for part in parts:
                size = part.size // groups
                outs.append(total[at : at + size].reshape(-1, part.shape[1]).astype(F32))
                at += size
            return outs

        source_attn, target_attn, cross_attn = [
            reduced(results.grads) for results in (source_back, target_back, cross)
        ]
        source_wide, target_wide = [reduced(results.grads[:2]) for results in (source_ffn, top)]

    def bias(first_row):
        if spread:
            return biases[first_row]
        whole = vectors[first_row : first_row + wide // width].reshape(groups, -1)
        return lax.dynamic_index_in_dim(whole, group, 0, keepdims=False)

    return (
        results[:, 0], results[:, 1], gradients[:, 0], gradients[:, 1],
        *source_attn, thin[7], thin[8],
        source_wide[0], bias(0), source_wide[1], thin[4], thin[5], thin[6],
        *target_attn, thin[18], thin[19],
        *cross_attn, thin[16], thin[17],
        target_wide[0], bias(9), target_wide[1], thin[13], thin[14], thin[15],
    )


def solution(mesh):
    rows = P("dp", "pipe", None)
    matrix, vector = P("dp", None), P("dp")
    in_specs = (rows, rows, P("dp"), P("dp"), rows, rows) + (P(),) * 27
    attention = (matrix, matrix, matrix, vector, vector)
    ffn = (matrix, vector, matrix, vector, vector, vector)
    out_specs = (rows,) * 4 + attention + ffn + attention + attention + ffn
    return jax.shard_map(shards, mesh=mesh, in_specs=in_specs, out_specs=out_specs, check_vma=False)
```

```python
import functools

import jax
import jax.numpy as jnp
from jax import lax
from jax.experimental import pallas as pl
from jax.experimental.pallas import tpu as pltpu
from jax.sharding import PartitionSpec as P

HEAD_DIM = 64
PAIR = 2 * HEAD_DIM
LOG2E = 1.4426950408889634
LN2 = 0.6931471805599453
HIDDEN = -1e30
BF = jnp.bfloat16
F32 = jnp.float32
VMEM_BYTES = 56 * 2**20
SMALL_BYTES = 16 * 2**20


def product(left, right, sides):
    return lax.dot_general(left, right, (sides, ((), ())), preferred_element_type=F32)


def nn(left, right):
    return product(left, right, ((1,), (0,)))


def nt(left, right):
    return product(left, right, ((1,), (1,)))


def tn(left, right):
    return product(left, right, ((0,), (0,)))


def norm_forward(value):
    center = value - jnp.mean(value, -1, keepdims=True)
    inverse = lax.rsqrt(jnp.mean(center * center, -1, keepdims=True) + 1e-05)
    return center * inverse, inverse


def norm_backward(gradient, normed, inverse, gain):
    scaled = gradient * gain
    back = inverse * (
        scaled
        - jnp.mean(scaled, -1, keepdims=True)
        - normed * jnp.mean(scaled * normed, -1, keepdims=True)
    )
    return (
        back,
        jnp.sum(gradient * normed, 0, keepdims=True),
        jnp.sum(gradient, 0, keepdims=True),
    )


def fill_bias(place_ref, count, causal, bias_ref):
    keys, width = bias_ref.shape
    rows = keys // 4
    for block in range(4):
        first = block * rows if causal else place_ref[block]
        at = first + lax.broadcasted_iota(jnp.int32, (rows, width), 0)
        allowed = at < count
        if causal:
            lane = lax.broadcasted_iota(jnp.int32, (rows, width), 1)
            asked = jnp.where(lane < rows, place_ref[0] + lane, place_ref[1] + lane - rows)
            allowed = allowed & (at <= asked)
        bias_ref[block * rows : (block + 1) * rows, :] = jnp.where(allowed, 0.0, HIDDEN)


def by_core(place_ref, rows, keys, run):
    block = rows // 2
    for core in range(2):
        seen = (core + 1, keys // block - core)

        @pl.when(place_ref[6] == core)
        def _(seen=seen):
            run(tuple((at * block, (at + 1) * block, count * block) for at, count in enumerate(seen)))


def bias_of(bias_ref, first, last, keys):
    width = bias_ref.shape[1]
    if width > 128:
        return bias_ref[:keys, first:last]
    return jnp.concatenate([bias_ref[:keys, :]] * ((last - first) // width), 1)


def head_lanes(half):
    lane = lax.broadcasted_iota(jnp.int32, (1, PAIR), 1)
    return (lane >= HEAD_DIM * half) & (lane < HEAD_DIM * (half + 1))


def project(own, other_ref, wq, wkv, q_ref, k_ref, v_ref, own_keys=None, starts=None):
    rows, width = own.shape
    q_ref[...] = (nn(own, wq[...]) * (HEAD_DIM**-0.5 * LOG2E)).astype(BF)
    keys = own if own_keys is None else own_keys
    for at in (0, rows):
        for ref, part in ((k_ref, wkv[:, :width]), (v_ref, wkv[:, width:])):
            value = nn(keys, part).astype(BF)
            if starts is None:
                ref[at : at + rows, :] = value
                continue
            block = rows // 2
            for half in range(2):
                first = pl.multiple_of(starts[2 * at // rows + half], block)
                ref[pl.ds(first, block), :] = value[half * block : (half + 1) * block]
        keys = other_ref[...]


def attend(spans, step, q_ref, k_ref, v_ref, bias_ref, ot_ref, lse_ref):
    def one_head(index, half):
        cols = pl.ds(pl.multiple_of(index // 2 * PAIR, PAIR), PAIR)
        at = pl.multiple_of(index * HEAD_DIM, HEAD_DIM)
        values = v_ref[:, cols].T
        if isinstance(half, int):
            values = values[HEAD_DIM * half : HEAD_DIM * (half + 1)]
        else:
            values = jnp.where(half == 0, values[:HEAD_DIM], values[HEAD_DIM:])
        for first, last, seen in spans:
            queries, keys = q_ref[first:last, cols], k_ref[:seen, cols]
            masked = jnp.where(head_lanes(half), queries, jnp.zeros_like(queries))
            scores = nt(keys, masked) + bias_of(bias_ref, first, last, seen)
            top = jnp.max(scores, 0, keepdims=True)
            expon = jnp.exp2(scores - top)
            total = jnp.sum(expon, 0, keepdims=True)
            mixed = nn(values[:, :seen], expon.astype(BF))
            ot_ref[pl.ds(at, HEAD_DIM), first:last] = mixed / total
            lse_ref[pl.ds(index, 1), first:last] = top + jnp.log2(total)

    def heads(index, carry):
        for half in range(step):
            one_head(step * index + half, half if step == 2 else index % 2)
        return carry

    lax.fori_loop(0, q_ref.shape[1] // HEAD_DIM // step, heads, 0)


def attend_back(
    spans, q_ref, k_ref, v_ref, do_ref, bias_ref, lse_ref, delta_ref, dqt_ref, dk_ref, dv_ref
):
    def pair(index, carry):
        cols = pl.ds(pl.multiple_of(index * PAIR, PAIR), PAIR)
        turned = k_ref[:, cols].T
        done = 0
        for first, last, seen in spans:
            keys, values = k_ref[:seen, cols], v_ref[:seen, cols]
            queries, grads = q_ref[first:last, cols], do_ref[first:last, cols]
            dkeys = dvalues = None
            for half in range(2):
                mine = head_lanes(half)
                masked = jnp.where(mine, queries, jnp.zeros_like(queries))
                masked_grads = jnp.where(mine, grads, jnp.zeros_like(grads))
                head = pl.ds(2 * index + half, 1)
                scores = nt(keys, masked) + bias_of(bias_ref, first, last, seen)
                probs = jnp.exp2(scores - lse_ref[head, first:last])
                dprobs = nt(values, masked_grads)
                dscores = (probs * (dprobs - delta_ref[head, first:last])).astype(BF)
                part = nn(probs.astype(BF), masked_grads)
                dvalues = part if half == 0 else dvalues + part
                part = nn(dscores, masked)
                dkeys = part if half == 0 else dkeys + part
                dquery = nn(turned[HEAD_DIM * half : HEAD_DIM * (half + 1), :seen], dscores)
                at = pl.multiple_of(index * PAIR + HEAD_DIM * half, HEAD_DIM)
                dqt_ref[pl.ds(at, HEAD_DIM), first:last] = (dquery * HEAD_DIM**-0.5).astype(BF)
            dkeys = dkeys * LN2
            if done:
                dkeys = jnp.concatenate([dkeys[:done] + dk_ref[:done, cols].astype(F32), dkeys[done:]], 0)
                dvalues = jnp.concatenate([dvalues[:done] + dv_ref[:done, cols].astype(F32), dvalues[done:]], 0)
            dk_ref[:seen, cols] = dkeys.astype(BF)
            dv_ref[:seen, cols] = dvalues.astype(BF)
            done = seen
        if done < k_ref.shape[0]:
            rest = jnp.zeros((k_ref.shape[0] - done, PAIR), BF)
            dk_ref[done:, cols] = rest
            dv_ref[done:, cols] = rest
        return carry

    lax.fori_loop(0, q_ref.shape[1] // PAIR, pair, 0)


class Spread:
    def __init__(self, core, keep_ref, send_ref):
        self.first = core == 0
        self.keep_ref, self.send_ref = keep_ref, send_ref
        self.quarters, self.planes, self.rows = keep_ref.shape[:3]

    def put(self, quarter, plane, at, even, odd):
        even, odd = even.astype(BF), odd.astype(BF)
        rows = slice(at, at + even.shape[0])
        self.keep_ref[quarter, plane, rows, :] = jnp.where(self.first, even, odd)
        self.send_ref[quarter, plane, rows, :] = jnp.where(self.first, odd, even)

    def square(self, value, at):
        chunk = value.shape[0] // (2 * self.planes)
        piece = chunk // self.quarters
        for plane in range(self.planes):
            for quarter in range(self.quarters):
                even = 2 * plane * chunk + quarter * piece
                odd = even + chunk
                self.put(quarter, plane, at, value[even : even + piece], value[odd : odd + piece])

    def columns(self, value, quarter, at):
        chunk = value.shape[0] // (2 * self.planes)
        for plane in range(self.planes):
            even = 2 * plane * chunk
            odd = even + chunk
            self.put(quarter, plane, at, value[even : even + chunk], value[odd : odd + chunk])

    def two_chunks(self, value, plane, at):
        chunk = value.shape[0] // 2
        piece = chunk // self.quarters
        for quarter in range(self.quarters):
            even = quarter * piece
            odd = even + chunk
            self.put(quarter, plane, at, value[even : even + piece], value[odd : odd + piece])

    def same(self, quarter, at, value):
        for plane in range(self.planes):
            self.put(quarter, plane, at, value, value)


class Chunks(Spread):
    def __init__(self, ref):
        self.ref = ref
        self.quarters, self.planes, self.rows = ref.shape[1], ref.shape[0] // 2, ref.shape[2]

    def put(self, quarter, plane, at, even, odd):
        rows = slice(at, at + even.shape[0])
        self.ref[2 * plane, quarter, rows, :] = even.astype(BF)
        self.ref[2 * plane + 1, quarter, rows, :] = odd.astype(BF)


class Whole:
    def __init__(self, refs):
        self.refs = refs


def spread_of(io, refs):
    if isinstance(refs, list) and len(refs) == 2:
        return Spread(io.place[6], *refs)
    if isinstance(refs, list):
        return Whole(refs)
    return Chunks(refs)


def spread_attention(spread, own, keys_own, keys_other, dar, ot_ref, dqt_ref, dk, dv):
    rows, width = dar.shape
    dq = dqt_ref[...].T
    own_t = own[...].T
    keys_t = own_t if keys_own is own else keys_own[...].T
    other_t = keys_other[...].T
    dwo = nn(ot_ref[...].astype(BF), dar)
    dwq = nn(own_t, dq)
    dwk = nn(keys_t, dk[0]) + nn(other_t, dk[1])
    dwv = nn(keys_t, dv[0]) + nn(other_t, dv[1])
    if isinstance(spread, Whole):
        wq_ref, wkv_ref, wo_ref = spread.refs
        wq_ref[...] = dwq.astype(BF)
        wkv_ref[:, :width] = dwk.astype(BF)
        wkv_ref[:, width:] = dwv.astype(BF)
        wo_ref[...] = dwo.astype(BF)
        return
    piece = spread.rows // 4
    for place, value in enumerate((dwq, dwk, dwv, dwo)):
        spread.square(value, place * piece)


BLOCK = 512
TANH_SCALE = 0.7978845608028654
TANH_CUBE = 0.044715


def expand(hidden, w1, b1, active_ref, slope_ref):
    for at in range(0, w1.shape[1], BLOCK):
        cols = slice(at, at + BLOCK)
        before = nn(hidden, w1[:, cols]) + b1[:, cols]
        square = before * before
        inner = before * (TANH_SCALE + (TANH_SCALE * TANH_CUBE) * square)
        curve = jnp.tanh(inner)
        half = 0.5 * (1.0 + curve)
        active_ref[:, cols] = (before * half).astype(BF)
        steep = TANH_SCALE + (3 * TANH_SCALE * TANH_CUBE) * square
        slope_ref[:, cols] = (half + (0.5 * before) * (1.0 - curve * curve) * steep).astype(BF)


def contract(hidden, residual, active_ref, w2, b2):
    total = hidden.astype(F32) + nn(active_ref[...], w2[...]) + b2[...] + residual.astype(F32)
    return norm_forward(total)


def ffn_backward(io, spread, back, hidden, parts, bias_grad_ref):
    low = back.astype(BF)
    hidden_t = hidden.T
    dhidden = None
    for number in range(bias_grad_ref.shape[0]):
        w1, w2, active, slope = parts(number)
        dactive = nt(low, w2).astype(BF)
        dbefore = (dactive.astype(F32) * slope.astype(F32)).astype(BF)
        bias_grad_ref[number : number + 1, :] = jnp.sum(dbefore.astype(F32), 0, keepdims=True)
        dcontract = tn(active, low)
        dexpand = nn(hidden_t, dbefore)
        if isinstance(spread, Whole):
            block = slice(number * BLOCK, (number + 1) * BLOCK)
            spread.refs[0][:, block] = dexpand.astype(BF)
            spread.refs[1][block, :] = dcontract.astype(BF)
        else:
            chunk = dexpand.shape[0] // (2 * spread.planes)
            spread.columns(dexpand, number, 0)
            spread.two_chunks(dcontract, number, chunk)
            io.send_part(spread.ref, 2 * number, (slice(None), number, slice(0, chunk)))
            pair = slice(2 * number, 2 * number + 2)
            io.send_part(spread.ref, 2 * number + 1, (pair, slice(None), slice(chunk, 2 * chunk)))
        part = nt(dbefore, w1)
        dhidden = part if dhidden is None else dhidden + part
    return dhidden, jnp.sum(low.astype(F32), 0, keepdims=True)


PARTS = 12


class Buffers:
    def __init__(self, place, ins, outs, small):
        self.place, self.ins, self.outs, self.small = place, ins, outs, small
        self.waiting, self.going = {}, []
        self.queue, late = [], []
        for name, entry in ins.items():
            if entry is None:
                self.ahead()
                continue
            buffer, sources, sems = entry
            copies = [
                pltpu.make_async_copy(source, buffer.at[where], sems.at[number])
                for number, (source, where) in enumerate(sources)
            ]
            self.waiting[name] = copies
            if len(copies) > 2:
                late.append(copies)
            else:
                self.queue += copies
        for copies in zip(*late, strict=True):
            self.queue += copies
        if None not in ins.values():
            self.ahead()
        self.sent = set()

    def __getattr__(self, name):
        if name in self.small:
            return self.small[name]
        if name in self.outs:
            buffers = self.outs[name]
            return [buffer for buffer, _, _ in buffers] if isinstance(buffers, list) else buffers[0]
        for copy in self.waiting[name]:
            self.wait(copy)
        self.waiting[name] = []
        return self.ins[name][0]

    def block(self, name, number):
        self.wait(self.waiting[name][number])
        if number + 1 == len(self.waiting[name]):
            self.waiting[name] = []
        return self.ins[name][0]

    def ahead(self):
        for copy in self.queue:
            copy.start()
        self.queue = []

    def wait(self, copy):
        if any(copy is other for other in self.queue):
            self.ahead()
        copy.wait()

    def results(self):
        for entry in self.outs.values():
            yield from entry if isinstance(entry, list) else [entry]

    def start(self, copy):
        copy.start()
        self.going.append(copy)

    def send(self, *refs):
        for buffer, targets, sems in self.results():
            if any(buffer is ref for ref in refs):
                self.sent.add(id(buffer))
                for number, (target, where) in enumerate(targets):
                    self.start(pltpu.make_async_copy(buffer.at[where], target, sems.at[number]))

    def send_part(self, ref, number, where):
        for buffer, targets, sems in self.results():
            if buffer is ref:
                self.sent.add(id(buffer))
                self.start(
                    pltpu.make_async_copy(buffer.at[where], targets[0][0].at[where], sems.at[number])
                )

    def finish(self):
        self.send(*[entry[0] for entry in self.results() if id(entry[0]) not in self.sent])
        for copies in self.waiting.values():
            for copy in copies:
                self.wait(copy)
        for copy in self.going:
            copy.wait()


class Part:
    def __init__(self, io, prefix):
        self.io, self.prefix = io, prefix
        self.place, self.send, self.ahead = io.place, io.send, io.ahead

    def __getattr__(self, name):
        return getattr(self.io, self.prefix + name)


class Ends(list):
    pass


class Blocks:
    def __init__(self, array, axis):
        self.array, self.axis = array, axis


def run(kernel, name, flops, place, ins, small, outs, scratch=(), vmem_bytes=VMEM_BYTES):
    arrays, buffers, sem_counts, shapes = [], [], [], []
    in_plan, out_plan = {}, {}

    def buffer(dims, dtype, sems):
        buffers.append(pltpu.VMEM(tuple(dims), dtype))
        sem_counts.append(sems)
        return len(buffers) - 1

    for key, value in ins.items():
        if value is None:
            in_plan[key] = None
            continue
        plan = []
        if isinstance(value, Blocks):
            array, axis = value.array, value.axis
            for at in range(0, array.shape[axis], BLOCK):
                where = (slice(None),) * axis + (slice(at, at + BLOCK),)
                plan.append((len(arrays), where, where))
            arrays.append(array)
            dims, dtype = array.shape, array.dtype
        else:
            rows = 0
            for part in value if isinstance(value, Ends) else [value]:
                array, index = part if isinstance(part, tuple) else (part, None)
                dims = array.shape if index is None else array.shape[1:]
                where = len(plan) if isinstance(value, Ends) else ()
                plan.append((len(arrays), () if index is None else (index,), where))
                rows += dims[0]
                arrays.append(array)
            dims, dtype = (rows, *dims[1:]), array.dtype
        in_plan[key] = (buffer(dims, dtype, len(plan)), plan)

    def plan_out(value):
        if isinstance(value, Ends):
            plan = [(len(shapes) + number, number) for number in range(len(value))]
            shapes.extend(value)
            rows = sum(part.shape[0] for part in value)
            return buffer((rows, *value[0].shape[1:]), value[0].dtype, len(plan)), plan
        shapes.append(value)
        return buffer(value.shape, value.dtype, PARTS), [(len(shapes) - 1, ())]

    for key, value in outs.items():
        whole = isinstance(value, list) and not isinstance(value, Ends)
        out_plan[key] = [plan_out(part) for part in value] if whole else plan_out(value)

    def body(place_ref, *refs):
        cuts = (len(small), len(arrays), len(shapes), len(buffers), len(sem_counts))
        groups, at = [], 0
        for count in cuts:
            groups.append(refs[at : at + count])
            at += count
        small_refs, in_refs, out_refs, buffer_refs, sems = groups

        def part_of(ref, where):
            return ref.at[where] if where else ref

        def settled(where, rows):
            if not isinstance(where, int):
                return where
            return (pl.ds(pl.multiple_of((place_ref[9] ^ where) * rows, rows), rows),)

        def out_entry(plan):
            number, targets = plan
            return (
                buffer_refs[number],
                [(out_refs[which], settled(where, out_refs[which].shape[0])) for which, where in targets],
                sems[number],
            )

        def in_entry(number, plan):
            parts = []
            for which, where, to in plan:
                source = part_of(in_refs[which], where)
                parts.append((source, settled(to, source.shape[0])))
            return buffer_refs[number], parts, sems[number]

        in_map = {key: plan and in_entry(*plan) for key, plan in in_plan.items()}
        out_map = {
            key: [out_entry(part) for part in plan] if isinstance(plan, list) else out_entry(plan)
            for key, plan in out_plan.items()
        }
        io = Buffers(place_ref, in_map, out_map, dict(zip(small, small_refs, strict=True)))
        kernel(io, *refs[at:])
        io.finish()

    vmem, anywhere = pl.BlockSpec(memory_space=pltpu.VMEM), pl.BlockSpec(memory_space=pl.ANY)
    moved = sum(a.size * a.dtype.itemsize for a in (*arrays, *shapes))
    results = pl.pallas_call(
        body,
        out_shape=shapes,
        in_specs=[pl.BlockSpec(memory_space=pltpu.SMEM)] + [vmem] * len(small) + [anywhere] * len(arrays),
        out_specs=[anywhere] * len(shapes),
        scratch_shapes=[*buffers, *[pltpu.SemaphoreType.DMA((count,)) for count in sem_counts], *scratch],
        name=name,
        cost_estimate=pl.CostEstimate(flops=flops, bytes_accessed=moved, transcendentals=0),
        compiler_params=pltpu.CompilerParams(vmem_limit_bytes=vmem_bytes),
    )(place, *small.values(), *arrays)

    def named(plan):
        if isinstance(plan, list):
            return [named(part) for part in plan]
        got = [results[which] for which, _ in plan[1]]
        return got if len(got) > 1 else got[0]

    return Results({key: named(plan) for key, plan in out_plan.items()})


class Results(dict):
    def __getattr__(self, name):
        return self[name]


def put_norm(io, normed, inverse, normed_ref, inverse_ref):
    normed_ref[...] = normed.astype(normed_ref.dtype)
    inverse_ref[...] = jnp.broadcast_to(inverse, inverse_ref.shape)
    io.send(normed_ref, inverse_ref)


def self_attention(io, count_at, causal, bias_ref):
    fill_bias(io.place, io.place[count_at], causal, bias_ref)
    rows = io.own[...]
    starts = [io.place[block] for block in range(4)] if causal else None
    project(rows, io.other, io.wq, io.wkv, io.q, io.k, io.v, starts=starts)
    io.send(io.q, io.k, io.v)
    io.ahead()
    q, k, v, ot, lse = io.q, io.k, io.v, io.ot, io.lse
    whole = ((0, q.shape[0], k.shape[0]),)
    attend(whole, 2, q, k, v, bias_ref, ot, lse)
    io.send(ot, lse)
    return tn(ot[...].astype(BF), io.wo[...]), rows


def run_spans(io, causal, run):
    rows, keys = io.q.shape[0], io.k.shape[0]
    if causal:
        by_core(io.place, rows, keys, run)
    else:
        run(((0, rows, keys),))


def encoder_forward_kernel(io, bias_ref):
    attn, rows = self_attention(io, 4, False, bias_ref)
    normed, inverse = norm_forward(rows.astype(F32) + attn)
    put_norm(io, normed, inverse, io.n0, io.i0)
    hidden = (normed * io.gain[...] + io.offset[...]).astype(BF)
    io.hidden[...] = hidden
    io.send(io.hidden)
    expand(hidden, io.w1, io.b1, io.active, io.slope)
    io.send(io.active, io.slope)
    normed, inverse = contract(hidden, rows, io.active, io.w2, io.b2)
    io.memory[...] = (normed * io.scale[...] + io.center[...]).astype(BF)
    io.send(io.memory)
    put_norm(io, normed, inverse, io.n1, io.i1)


def decoder_forward_kernel(io, causal_ref, bias_ref, active_ref, slope_ref):
    attn, rows = self_attention(Part(io, "s"), 5, True, causal_ref)
    normed, inverse = norm_forward(rows.astype(F32) + attn)
    put_norm(io, normed, inverse, io.n, io.i)
    spread = spread_of(io, io.grads)
    fill_bias(io.place, io.place[4], False, bias_ref)
    first = normed * io.gain[...] + io.offset[...]
    first_low = first.astype(BF)
    io.first[...] = first_low
    io.send(io.first)
    memory = io.mem_own[...]
    project(first_low, io.mem_other, io.wq, io.wkv, io.q, io.k, io.v, memory)
    io.send(io.q, io.k, io.v)
    io.ahead()
    q, k, v, ot, lse = io.q, io.k, io.v, io.ot, io.lse
    whole = ((0, q.shape[0], k.shape[0]),)
    attend(whole, 2, q, k, v, bias_ref, ot, lse)
    io.send(io.ot, io.lse)
    n2, i2 = norm_forward(first + tn(io.ot[...].astype(BF), io.wo[...]))
    second = (n2 * io.cross_gain[...] + io.cross_offset[...]).astype(BF)
    expand(second, io.w1, io.b1, active_ref, slope_ref)
    n3, i3 = contract(second, io.sown[...], active_ref, io.w2, io.b2)
    output = (n3 * io.scale[...] + io.center[...]).astype(BF)
    block = output.shape[0] // 2
    for half in range(2):
        rows = slice(half * block, (half + 1) * block)
        io.result[2 * half] = memory[rows]
        io.result[2 * half + 1] = output[rows]
    io.send(io.result)
    back, dscale, dcenter = norm_backward(io.cotangent[...].astype(F32), n3, i3, io.scale[...])
    io.dr[...] = back.astype(BF)
    io.send(io.dr)
    w1, w2 = io.w1, io.w2

    def parts(number):
        cut = slice(number * BLOCK, (number + 1) * BLOCK)
        return w1[:, cut], w2[cut, :], active_ref[:, cut], slope_ref[:, cut]

    vecs = io.vecs
    dhidden, dshift = ffn_backward(io, spread, back, second, parts, vecs.at[0:4])
    dsecond = (back + dhidden).astype(BF).astype(F32)
    dv2, dgain, doffset = norm_backward(dsecond, n2, i2, io.cross_gain[...])
    io.dv[...] = dv2
    io.send(io.dv)
    put_rows(vecs, 4, (dshift, dscale, dcenter, dgain, doffset))


def put_rows(ref, at, values):
    for row, value in enumerate(values):
        ref[at + row : at + row + 1, :] = value
    at += len(values)
    ref[at:, :] = jnp.zeros((ref.shape[0] - at, ref.shape[1]), F32)


def cross_backward_kernel(io, bias_ref, *scratch):
    fill_bias(io.place, io.place[4], False, bias_ref)
    dv2 = io.dv[...]
    du, dc_own, dc_other = attention_backward(
        io, False, bias_ref, scratch, dv2.astype(BF), "first", "mem_own", "mem_other"
    )
    io.dmem_other[...] = dc_other.astype(BF)
    io.dmem_own[...] = dc_own.astype(BF)
    io.send(io.dmem_other, io.dmem_own)
    dv1, dgain, doffset = norm_backward(dv2 + du, io.n[...].astype(F32), io.i[:, :1], io.gain[...])
    io.dv1[...] = dv1
    io.send(io.dv1)
    put_rows(io.vecs, 0, (dgain, doffset))


def self_backward(io, count_at, causal, bias_ref, scratch):
    fill_bias(io.place, io.place[count_at], causal, bias_ref)
    dv = io.dv[...]
    du, dc_own, dc_other = attention_backward(
        io, causal, bias_ref, scratch, dv.astype(BF), "own", "own", "other"
    )
    io.dc_other[...] = dc_other.astype(BF)
    io.send(io.dc_other)
    io.du[...] = (dv + io.extra[...].astype(F32) + du + dc_own).astype(BF)
    io.send(io.du)


def source_backward_kernel(io, bias_ref, *scratch):
    self_backward(io, 4, False, bias_ref, scratch)


def target_backward_kernel(io, bias_ref, *scratch):
    self_backward(io, 5, True, bias_ref, scratch)


def attention_backward(io, causal, bias_ref, scratch, dar, own, keys_own, keys_other):
    spread = spread_of(io, io.grads)
    do_ref, delta_ref, dqt_ref, dk_ref, dv_ref = scratch
    rows, width = dar.shape
    wo, ot = io.wo, io.ot
    do_ref[...] = nt(dar, wo[...]).astype(BF)
    turned = nt(wo[...], dar).astype(BF).astype(F32) * ot[...]
    delta_ref[...] = jnp.sum(turned.reshape(width // HEAD_DIM, HEAD_DIM, rows), 1)
    queries, keys, values, lse = io.q, io.k, io.v, io.lse
    io.ahead()
    run_spans(
        io,
        causal,
        lambda spans: attend_back(
            spans, queries, keys, values, do_ref, bias_ref, lse, delta_ref, dqt_ref, dk_ref, dv_ref
        ),
    )
    if causal:
        starts = [io.place[block] for block in range(4)]
        dk, dv = [
            [
                jnp.concatenate([ref[pl.ds(pl.multiple_of(first, rows // 2), rows // 2), :] for first in firsts], 0)
                for firsts in (starts[:2], starts[2:])
            ]
            for ref in (dk_ref, dv_ref)
        ]
    else:
        dk, dv = [[ref[:rows, :], ref[rows:, :]] for ref in (dk_ref, dv_ref)]
    own_ref = getattr(io, own)
    keys_ref = own_ref if keys_own == own else getattr(io, keys_own)
    spread_attention(spread, own_ref, keys_ref, getattr(io, keys_other), dar, ot, dqt_ref, dk, dv)
    io.send(*io.grads)
    dq = dqt_ref[...].T
    wkv = io.wkv
    dc = [
        nt(dk[at], wkv[:, :width]) + nt(dv[at], wkv[:, width:])
        for at in (1, 0)
    ]
    return nt(dq, io.wq[...]), dc[1], dc[0]


def encoder_ffn_backward(io):
    spread = spread_of(io, io.grads)
    dmemory = (io.dmem_own[...].astype(F32) + io.dmem_came[...].astype(F32)).astype(BF).astype(F32)
    total = io.cotangent[...].astype(F32) + dmemory
    back, dscale, dcenter = norm_backward(total, io.n1[...].astype(F32), io.i1[:, :1], io.scale[...])
    io.dr[...] = back.astype(BF)
    io.send(io.dr)

    def parts(number):
        cut = slice(number * BLOCK, (number + 1) * BLOCK)
        return (
            io.block("w1", number)[:, cut],
            io.block("w2", number)[cut, :],
            io.block("active", number)[:, cut],
            io.block("slope", number)[:, cut],
        )

    vecs = io.vecs
    dhidden, dshift = ffn_backward(io, spread, back, io.hidden[...], parts, vecs.at[0:4])
    dlow = (back + dhidden).astype(BF).astype(F32)
    dv0, dgain, doffset = norm_backward(dlow, io.n0[...].astype(F32), io.i0[:, :1], io.gain[...])
    io.dv[...] = dv0
    io.send(io.dv)
    top, cross = io.top_vecs, io.cross_vecs
    rest = [top[row : row + 1, :] for row in range(9)] + [cross[row : row + 1, :] for row in range(2)]
    put_rows(vecs, 4, (dshift, dscale, dcenter, dgain, doffset, *rest))
    if not isinstance(spread, Whole):
        share = vecs.shape[0] // spread.quarters
        for quarter in range(spread.quarters):
            spread.same(quarter, spread.rows - share, vecs[quarter * share : (quarter + 1) * share, :])
        where = (slice(None), slice(None), slice(spread.rows - share, spread.rows))
        io.send_part(spread.ref, PARTS - 1, where)


def small_kernel(body, name, outs, place, *args):
    vmem = pl.BlockSpec(memory_space=pltpu.VMEM)
    moved = sum(a.size * a.dtype.itemsize for a in (*args, *outs))
    return pl.pallas_call(
        body,
        out_shape=outs,
        in_specs=[pl.BlockSpec(memory_space=pltpu.SMEM)] + [vmem] * len(args),
        out_specs=[vmem] * len(outs),
        name=name,
        cost_estimate=pl.CostEstimate(flops=0, bytes_accessed=moved, transcendentals=0),
        compiler_params=pltpu.CompilerParams(vmem_limit_bytes=SMALL_BYTES),
    )(place, *args)


def split_kernel(pairs, extra, place_ref, *refs):
    outs = refs[2 * pairs + extra :]
    for step, out_ref in enumerate(outs):
        quarter = place_ref[7] ^ step
        at = 0
        for plane in range(refs[0].shape[1]):
            for pair in range(pairs):
                keep_ref, came_ref = refs[2 * pair : 2 * pair + 2]
                rows = keep_ref.shape[2]
                total = keep_ref[quarter, plane].astype(F32) + came_ref[quarter, plane].astype(F32)
                out_ref[at : at + rows, :] = total.astype(BF)
                at += rows
        if extra:
            out_ref[at:, :] = refs[2 * pairs][quarter]


def split_pieces(place, pairs, extra=None):
    quarters, planes, _, width = pairs[0][0].shape
    rows = planes * sum(keep.shape[2] for keep, _ in pairs)
    args = [part for pair in pairs for part in pair]
    if extra is not None:
        rows += extra.shape[1]
        args.append(extra)
    body = functools.partial(split_kernel, len(pairs), int(extra is not None))
    outs = [jax.ShapeDtypeStruct((rows, width), BF)] * quarters
    return list(small_kernel(body, "split", outs, place, *args))


def join_kernel(place_ref, whole_ref, pieces_ref, *outs):
    rows = whole_ref.shape[0]
    for step, out_ref in enumerate(outs):
        out_ref[:rows, :] = whole_ref[...]
        out_ref[rows:, :] = pieces_ref[place_ref[7] ^ step]


def join_pieces(place, whole, pieces):
    outs = [jax.ShapeDtypeStruct((whole.shape[0] + pieces.shape[1], whole.shape[1]), BF)] * pieces.shape[0]
    return list(small_kernel(join_kernel, "join", outs, place, whole, pieces))


def home_kernel(place_ref, *refs):
    dus, came_refs, outs = (refs[:2], refs[2:4]), refs[4:6], refs[6:]
    rows = outs[0].shape[1]
    for which, out_ref in enumerate(outs):
        at = pl.multiple_of((place_ref[9] ^ which) * rows, rows)
        for number, (du, came_ref) in enumerate(zip(dus, came_refs, strict=True)):
            out_ref[number] = (du[which][...].astype(F32) + came_ref[pl.ds(at, rows), :].astype(F32)).astype(BF)


def home_blocks(place, source_du, source_came, target_du, target_came):
    outs = [jax.ShapeDtypeStruct((2, *source_du[0].shape), BF)] * 2
    return list(small_kernel(home_kernel, "home", outs, place, *source_du, *target_du, source_came, target_came))


def fold_kernel(sets, planes, with_ready, place_ref, *refs):
    parts, outs = refs[:-planes], refs[-planes:]
    above = 0
    if with_ready:
        ready, parts = parts[-planes:], parts[:-planes]
        above = ready[0].shape[0]
    quarters, rows = len(parts) // sets, (outs[0].shape[0] - above) // sets
    for step, out_ref in enumerate(outs):
        if with_ready:
            out_ref[:above, :] = ready[step][...]
        plane = (place_ref[8] // 2) ^ step
        where = pl.ds(pl.multiple_of(plane * rows, rows), rows)
        for number in range(sets):
            of_set = parts[number * quarters : (number + 1) * quarters]
            total = sum(part[where, :].astype(F32) for part in of_set)
            at = above + number * rows
            out_ref[at : at + rows, :] = total.astype(BF)


def fold_pieces(place, sets, planes, height, ready=()):
    rows = len(sets) * height // planes + (ready[0].shape[0] if ready else 0)
    outs = [jax.ShapeDtypeStruct((rows, sets[0][0].shape[1]), BF)] * planes
    body = functools.partial(fold_kernel, len(sets), planes, bool(ready))
    return list(small_kernel(body, "fold", outs, place, *[part for parts in sets for part in parts], *ready))


def unpack_kernel(plan, io):
    chip, group = io.place[7], io.place[8]
    pieces = [ref for key, ref in io.small.items()]
    if len(pieces) == 1:
        pieces = [(quarter, pieces[0].at[quarter]) for quarter in range(pieces[0].shape[0])]
    else:
        pieces = [(chip ^ step, ref) for step, ref in enumerate(pieces)]
    quarters = len(pieces)
    for quarter, piece_ref in pieces:
        width = piece_ref.shape[1]
        at = 0
        for kind, outs in plan:
            refs = getattr(io, outs)
            if kind == ATTENTION:
                size = refs[0].shape[0] // quarters
                rows = pl.ds(pl.multiple_of(quarter * size, size), size)
                values = [piece_ref[at + i * size : at + (i + 1) * size, :].astype(F32) for i in range(4)]
                refs[0][rows, :] = values[0]
                refs[1][rows, :width] = values[1]
                refs[1][rows, width:] = values[2]
                refs[2][rows, :] = values[3]
                at += 4 * size
            elif kind == FEEDFORWARD:
                size = refs[0].shape[0]
                cols = pl.ds(pl.multiple_of(quarter * width, width), width)
                refs[0][:, cols] = piece_ref[at : at + size, :].astype(F32)
                at += size
                size = refs[1].shape[0] // quarters
                rows = pl.ds(pl.multiple_of(quarter * size, size), size)
                refs[1][rows, :] = piece_ref[at : at + size, :].astype(F32)
                at += size
            else:
                size = piece_ref.shape[0] - at
                rows = pl.ds(pl.multiple_of(quarter * size, size), size)
                refs[0][rows, :] = piece_ref[at:, :].astype(F32)
    if kind == VECTORS:
        short = refs[1].shape[0]
        pair = refs[0][:, pl.ds(pl.multiple_of((group // 2) * 2 * short, 2 * short), 2 * short)]
        thin = jnp.where(group % 2 == 0, pair[:, :short], pair[:, short:])
        for number, at in enumerate(THIN_ROWS):
            refs[1 + number][...] = thin[at]
        long = 4 * short
        lanes = pl.ds(pl.multiple_of((group % 2) * long, long), long)
        for number, at in enumerate(LONG_ROWS):
            refs[1 + len(THIN_ROWS) + number][...] = refs[0][pl.ds(at + group // 2, 1), lanes][0]


ATTENTION, FEEDFORWARD, VECTORS = range(3)
THIN_ROWS = (4, 5, 6, 7, 8, 13, 14, 15, 16, 17, 18, 19)
LONG_ROWS = (0, 9)


class Places:
    def __init__(self, quarters, groups):
        self.quarters, self.groups = quarters, groups
        self.sends = []
        for which in range(2):
            pairs = []
            for quarter in range(quarters):
                for group in range(groups):
                    plane, core = divmod(group, 2)
                    worker = self.chip_of(core, self.place_of(quarter) ^ which)
                    target = worker * groups + 2 * plane + self.group_of(quarter)
                    pairs.append((quarter * groups + group, target))
            self.sends.append(pairs)
        self.cores = [(group, group ^ 1) for group in range(groups)]

    def group_of(self, quarter):
        return (quarter ^ (quarter >> 1)) & 1

    def place_of(self, quarter):
        return quarter >> 1

    def chip_of(self, group, place):
        return 2 * place + (group ^ place)

    def order(self, rows, upper):
        return [jnp.where(upper, rows[1], rows[0]), jnp.where(upper, rows[0], rows[1])]

    def to_work(self, parts):
        return [
            lax.ppermute(part, ("pipe", "dp"), pairs)
            for part, pairs in zip(parts, self.sends, strict=True)
        ]

    def to_home(self, block_a, block_b):
        return [
            lax.ppermute(part, ("pipe", "dp"), pairs)
            for part, pairs in zip((block_a, block_b), self.sends, strict=True)
        ]

    def at_home(self, came, upper):
        first, second = came
        return jnp.stack([jnp.where(upper, second, first), jnp.where(upper, first, second)])

    def to_other_core(self, value):
        return lax.ppermute(value, "dp", self.cores)


def gate(*values):
    return list(lax.optimization_barrier(values))


def together(*values):
    return lax.optimization_barrier(values)


def after(results, *flying):
    kept, flying = lax.optimization_barrier((dict(results), flying))
    return Results(kept), *flying


def to_quarters(parts):
    quarters = len(parts)
    return [
        part if step == 0 else lax.ppermute(part, "pipe", [(i, i ^ step) for i in range(quarters)])
        for step, part in enumerate(parts)
    ]


def to_planes(parts):
    groups = 2 * len(parts)
    return [
        part if step == 0 else lax.ppermute(part, "dp", [(i, i ^ (2 * step)) for i in range(groups)])
        for step, part in enumerate(parts)
    ]


def total_of(parts):
    return sum(part.astype(F32) for part in parts).astype(BF)


def by_step(value, index):
    return [
        lax.dynamic_index_in_dim(value, index ^ step, 0, keepdims=False) for step in range(value.shape[0])
    ]


def shards(
    source, target, source_length, target_length, memory_cotangent, output_cotangent,
    source_query, source_keyvalue, source_output, source_gain, source_offset,
    source_expand, source_bias, source_contract, source_shift, source_scale, source_center,
    target_query, target_keyvalue, target_output, target_gain, target_offset,
    cross_query, cross_keyvalue, cross_output, cross_gain, cross_offset,
    target_expand, target_bias, target_contract, target_shift, target_scale, target_center,
):
    quarters, groups = lax.axis_size("pipe"), lax.axis_size("dp")
    chip, group = lax.axis_index("pipe"), lax.axis_index("dp")
    core, planes = group % 2, groups // 2
    micro, block, width = source.shape
    rows, keys = 2 * block, 4 * block
    heads = width // HEAD_DIM
    wide = source_expand.shape[1]
    spread = (width // groups) % (16 * quarters) == 0
    places = Places(quarters, groups)
    upper = chip >= quarters // 2
    swap = places.to_other_core

    lengths = jnp.stack([source_length, target_length])
    other_lengths = swap(lengths)
    own = places.to_work(places.order(source, upper))
    counts = jnp.where(core == places.group_of(chip), lengths, other_lengths)
    counts = lax.dynamic_index_in_dim(counts, places.place_of(chip), 1, keepdims=False)
    starts = [places.chip_of(which, at) * block for which in (core, 1 - core) for at in range(2)]
    slots = [*starts, counts[0], counts[1], core, chip, group, places.place_of(chip)]
    place = jnp.stack([jnp.asarray(slot, jnp.int32) for slot in slots])
    late = places.order(jnp.stack([target, output_cotangent, memory_cotangent], 1), upper)
    own, late, place = together(own, late, place)
    other = Ends(swap(part) for part in own)
    own = Ends(own)
    late = places.to_work(late)


    def row(vector):
        return vector.reshape(1, -1)

    def shape(*dims, dtype=BF):
        return jax.ShapeDtypeStruct(dims, dtype)

    half = shape(block, width)
    sheet = shape(rows, width, dtype=F32)
    lanes = shape(rows, 128, dtype=F32)
    saved = Results(
        q=shape(rows, width), k=shape(keys, width), v=shape(keys, width),
        ot=shape(width, rows, dtype=F32), lse=shape(heads, rows, dtype=F32),
    )
    flat_bias = pltpu.VMEM((keys, 128), F32)
    causal_bias = pltpu.VMEM((keys, rows), F32)
    back_scratch = [
        pltpu.VMEM((rows, width), BF), pltpu.VMEM((heads, rows), F32), pltpu.VMEM((width, rows), BF),
        pltpu.VMEM((keys, width), BF), pltpu.VMEM((keys, width), BF),
    ]
    vec_rows = 16 * quarters
    if spread:
        attn_rows = 4 * width // (groups * quarters)
        ffn_rows = 2 * wide // (groups * quarters)
        attention_grads = [shape(quarters, planes, attn_rows, width)] * 2
        top_grads = shape(groups, quarters, ffn_rows, width)
        source_ffn_grads = shape(groups, quarters, ffn_rows + vec_rows // quarters, width)
    else:
        attention_grads = [shape(width, cols) for cols in (width, 2 * width, width)]
        top_grads = [shape(width, wide), shape(wide, width), shape(16, 128)]
        source_ffn_grads = top_grads
    core_flops = 2 * 4 * rows * keys * width
    linear_flops = 2 * rows * width * width
    ffn_flops = 4 * rows * width * wide
    attn_flops = 2 * core_flops + 8 * linear_flops
    attn_back_flops = 5 * core_flops + 16 * linear_flops

    encoder = run(
        encoder_forward_kernel, "encoder", attn_flops + ffn_flops, place,
        dict(own=own, wq=source_query, other=other, wkv=source_keyvalue, rest=None, wo=source_output, w1=source_expand,
             w2=source_contract),
        dict(gain=row(source_gain), offset=row(source_offset), b1=row(source_bias), b2=row(source_shift),
             scale=row(source_scale), center=row(source_center)),
        dict(**saved, n0=shape(rows, width), i0=lanes, hidden=shape(rows, width), active=shape(rows, wide),
             slope=shape(rows, wide), n1=shape(rows, width), i1=lanes, memory=shape(rows, width)),
        [flat_bias],
    )
    *late, memory = gate(*late, encoder.memory)
    target_own = Ends((part, 0) for part in late)
    target_other = Ends(swap(part[0]) for part in late)
    memory_other = swap(memory)
    top = run(
        decoder_forward_kernel, "decoder", 2 * attn_flops + 3 * ffn_flops, place,
        dict(sown=target_own, swq=target_query, sother=target_other, swkv=target_keyvalue, rest=None, swo=target_output,
             wq=cross_query, mem_own=memory, mem_other=memory_other, wkv=cross_keyvalue, wo=cross_output,
             w1=target_expand, w2=target_contract, cotangent=Ends((part, 1) for part in late)),
        dict(gain=row(target_gain), offset=row(target_offset), cross_gain=row(cross_gain),
             cross_offset=row(cross_offset), b1=row(target_bias), b2=row(target_shift), scale=row(target_scale),
             center=row(target_center)),
        dict(sq=saved.q, sk=saved.k, sv=saved.v, sot=saved.ot, slse=saved.lse, n=shape(rows, width), i=lanes, **saved,
             first=shape(rows, width), result=Ends([shape(2, block, width)] * 2), dr=shape(rows, width), dv=sheet,
             vecs=shape(16, width, dtype=F32), grads=top_grads),
        [causal_bias, flat_bias, pltpu.VMEM((rows, wide), BF), pltpu.VMEM((rows, wide), BF)],
    )
    results = places.to_home(*top.result)
    if spread:
        top_total = lax.psum_scatter(top.grads, "dp", scatter_dimension=0, tiled=True)[0]

    def kept(results):
        return dict(ot=results.ot, k=results.k, q=results.q, v=results.v, lse=results.lse, rest=None)

    decoder = Results(ot=top.sot, k=top.sk, q=top.sq, v=top.sv, lse=top.slse)

    cross = run(
        cross_backward_kernel, "cross_back", attn_back_flops, place,
        dict(dv=top.dv, wo=cross_output, **kept(top), first=top.first, mem_own=memory, mem_other=memory_other,
             wkv=cross_keyvalue, wq=cross_query, n=top.n, i=top.i),
        dict(gain=row(target_gain)),
        dict(dmem_own=shape(rows, width), dmem_other=shape(rows, width), dv1=sheet, vecs=shape(8, width, dtype=F32),
             grads=attention_grads),
        [flat_bias, *back_scratch],
    )
    cross, results = after(cross, results)
    results = places.at_home(results, upper)
    dmem_came = swap(cross.dmem_other)
    cross_came = swap(cross.grads[1]) if spread else ()
    target_back = run(
        target_backward_kernel, "target_back", attn_back_flops, place,
        dict(dv=cross.dv1, wo=target_output, **kept(decoder), own=target_own, other=target_other,
             wkv=target_keyvalue, wq=target_query, extra=top.dr),
        {}, dict(dc_other=shape(rows, width), du=Ends([half, half]), grads=attention_grads),
        [causal_bias, *back_scratch],
    )
    target_back, dmem_came, cross_came = after(target_back, dmem_came, cross_came)
    dtarget_came = swap(target_back.dc_other)
    target_came, early = (), ()
    if spread:
        target_came = swap(target_back.grads[1])
        early = split_pieces(place, [(cross.grads[0], cross_came)])
        early, dmem_came = together(early, dmem_came)
        early = to_quarters(early)
    source_ffn = run(
        encoder_ffn_backward, "source_ffn", 2 * ffn_flops, place,
        dict(cotangent=Ends((part, 2) for part in late), dmem_own=cross.dmem_own, dmem_came=dmem_came,
             n1=encoder.n1, i1=encoder.i1, w2=Blocks(source_contract, 0), slope=Blocks(encoder.slope, 1),
             w1=Blocks(source_expand, 1), active=Blocks(encoder.active, 1), hidden=encoder.hidden, n0=encoder.n0,
             i0=encoder.i0),
        dict(scale=row(source_scale), gain=row(source_gain), top_vecs=top.vecs, cross_vecs=cross.vecs),
        dict(dr=shape(rows, width), dv=sheet, vecs=shape(vec_rows, width, dtype=F32), grads=source_ffn_grads),
    )
    source_ffn, dtarget_came, target_came, early = after(source_ffn, dtarget_came, target_came, early)
    dv0, middle = source_ffn.dv, ()
    if spread:
        source_total = lax.psum_scatter(source_ffn.grads, "dp", scatter_dimension=0, tiled=True)[0]
        middle = split_pieces(place, [(target_back.grads[0], target_came)], top_total)
        dv0, middle = together(dv0, middle)
        middle = to_quarters(middle)
    source_back = run(
        source_backward_kernel, "source_back", attn_back_flops, place,
        dict(dv=dv0, wo=source_output, **kept(encoder), own=own, other=other, wkv=source_keyvalue,
             wq=source_query, extra=source_ffn.dr),
        {}, dict(dc_other=shape(rows, width), du=Ends([half, half]), grads=attention_grads),
        [flat_bias, *back_scratch],
    )
    source_back, middle = after(source_back, middle)

    def attention_outs():
        chunk = width // groups
        return [shape(chunk, width, dtype=F32), shape(chunk, 2 * width, dtype=F32), shape(chunk, width, dtype=F32)]

    def ffn_outs():
        return [shape(width // groups, wide, dtype=F32), shape(wide // groups, width, dtype=F32)]

    def unpack(name, plan, parts, outs):
        return run(
            functools.partial(unpack_kernel, plan), name, 0, place, {}, dict(enumerate(parts)), outs, vmem_bytes=SMALL_BYTES
        )

    dc_other = source_back.dc_other
    if spread:
        last_came = swap(source_back.grads[1])
        last = split_pieces(place, [(source_back.grads[0], last_came)])
        height = planes * attn_rows
        home = home_blocks(place, source_back.du, swap(dc_other), target_back.du, dtarget_came)
        last, home = together(last, home)
        last, home = to_quarters(last), places.to_home(*home)
        first = total_of([part[height:] for part in middle])
        ready = fold_pieces(place, [early, middle], planes, height)
        both = to_planes(fold_pieces(place, [last], planes, height, ready))
        pieces = to_quarters(join_pieces(place, first, source_total))
        both, pieces, home = together(both, pieces, home)
        first = pieces
        pieces = [part[ffn_rows:] for part in pieces]
        last = [jnp.concatenate([total_of(both), total_of(pieces)], 0)] * quarters
        last = to_quarters(last)
    else:
        home = home_blocks(place, source_back.du, swap(dc_other), target_back.du, dtarget_came)
        home = places.to_home(*home)
    gradients = places.at_home(home, upper).astype(F32)
    if spread:
        first_grads = unpack(
            "unpack_first", ((FEEDFORWARD, "top"),), first, dict(top=ffn_outs()),
        )
        last_grads = unpack(
            "unpack_last",
            (
                (ATTENTION, "cross"), (ATTENTION, "target"), (ATTENTION, "source"), (FEEDFORWARD, "low"),
                (VECTORS, "vectors"),
            ),
            last,
            dict(cross=attention_outs(), target=attention_outs(), source=attention_outs(), low=ffn_outs(),
                 vectors=[shape(vec_rows, width, dtype=F32)] + [shape(width // groups, dtype=F32)] * len(THIN_ROWS)
                 + [shape(wide // groups, dtype=F32)] * len(LONG_ROWS)),
        )
        thin = dict(zip(THIN_ROWS, last_grads.vectors[1:], strict=False))
        biases = dict(zip(LONG_ROWS, last_grads.vectors[-len(LONG_ROWS) :], strict=True))
        source_attn, target_attn, cross_attn = last_grads.source, last_grads.target, last_grads.cross
        source_wide, target_wide = last_grads.low, first_grads.top
    else:
        vectors = lax.psum(source_ffn.vecs, ("pipe", "dp"))
        thin = lax.dynamic_slice_in_dim(vectors, group * (width // groups), width // groups, 1)

        def reduced(parts):
            flat = jnp.concatenate([part.reshape(groups, -1) for part in parts], 1)
            total = lax.psum(lax.psum_scatter(flat, "dp", scatter_dimension=0, tiled=True)[0], "pipe")
            outs, at = [], 0
            for part in parts:
                size = part.size // groups
                outs.append(total[at : at + size].reshape(-1, part.shape[1]).astype(F32))
                at += size
            return outs

        source_attn, target_attn, cross_attn = [
            reduced(results.grads) for results in (source_back, target_back, cross)
        ]
        source_wide, target_wide = [reduced(results.grads[:2]) for results in (source_ffn, top)]

    def bias(first_row):
        if spread:
            return biases[first_row]
        whole = vectors[first_row : first_row + wide // width].reshape(groups, -1)
        return lax.dynamic_index_in_dim(whole, group, 0, keepdims=False)

    return (
        results[:, 0], results[:, 1], gradients[:, 0], gradients[:, 1],
        *source_attn, thin[7], thin[8],
        source_wide[0], bias(0), source_wide[1], thin[4], thin[5], thin[6],
        *target_attn, thin[18], thin[19],
        *cross_attn, thin[16], thin[17],
        target_wide[0], bias(9), target_wide[1], thin[13], thin[14], thin[15],
    )


def solution(mesh):
    rows = P("dp", "pipe", None)
    matrix, vector = P("dp", None), P("dp")
    in_specs = (rows, rows, P("dp"), P("dp"), rows, rows) + (P(),) * 27
    attention = (matrix, matrix, matrix, vector, vector)
    ffn = (matrix, vector, matrix, vector, vector, vector)
    out_specs = (rows,) * 4 + attention + ffn + attention + attention + ffn
    return jax.shard_map(shards, mesh=mesh, in_specs=in_specs, out_specs=out_specs, check_vma=False)
```
